256 devices in a mesh: lon: 16 (over x, y_lo, core), lat: 16 (over y_hi, z).
Axes of the slice: x: 4, y: 4 (y_hi: 2, y_lo: 2; y = y_hi * 2 + y_lo), z: 8, core: 2. Of those that a mesh axis runs over, the one named last changes fastest.
Arguments:
- thermal_state: float32 [8, 2048, 4096], P(None, 'lat', 'lon'), may hold values from -6 to 6
- zonal_boundary_speed: float32 [8, 2048, 4096], P(None, 'lat', 'lon'), may hold values from -6 to 6
- meridional_boundary_speed: float32 [8, 2048, 4096], P(None, 'lat', 'lon'), may hold values from -6 to 6
- sea_indicator_grid: int32 [8, 2048, 4096], P(None, 'lat', 'lon'), may hold values from 0 to 1, as said below
- bathymetry_depth_index: int32 [2048, 4096], P('lat', 'lon'), may hold values from 0 to 8, as said below
- revised_thermal_adjoint: float32 [8, 2048, 4096], P(None, 'lat', 'lon'), may hold values from -6 to 6
- input_stratum_matrix: float32 [128, 32], replicated, may hold values from -1 to 1
- input_stratum_offset: float32 [128], replicated, may hold values from -3 to 3
- hidden_stratum_matrix: float32 [128, 128], replicated, may hold values from -0.5 to 0.5
- hidden_stratum_offset: float32 [128], replicated, may hold values from -3 to 3
- output_stratum_matrix: float32 [8, 128], replicated, may hold values from -0.5 to 0.5
- output_stratum_offset: float32 [8], replicated, may hold values from -4 to 4
Outputs:
- revised_thermal_state: float32 [8, 2048, 4096], P(None, 'lat', 'lon')
- surface_height: float32 [2048, 4096], P('lat', 'lon')
- inner_weight_gradient: float32 [128, 32], replicated
- inner_bias_gradient: float32 [128], replicated
- hidden_weight_gradient: float32 [128, 128], replicated
- hidden_bias_gradient: float32 [128], replicated
- outer_weight_gradient: float32 [8, 128], replicated
- outer_bias_gradient: float32 [8], replicated
The draws below stay inside these ranges and needn't reach their ends.
Inputs may be any that keep to these rules, and one draw needn't show every extreme that they name: sea_indicator_grid is 1 only at levels below the column's bathymetry_depth_index. `bathymetry_depth_index`: levels of each column; 0 is land.
All inputs are finite; a program needn't handle non-finite values.
Results may differ from the reference program's by a relative error of at most 0.0071.
The reference program's roundings to bfloat16 on the way (of `features`, `first_stored` and `second_stored`) count: a program that leaves them out, or rounds other values in their place, can miss the bound.
Values sent between devices are 32-bit elements; how exact they have to be, the bound alone decides.
No kernel may reach another device: no remote copies, remote signals or barrier semaphores. Data moves between devices by JAX's collectives and lax.ppermute only.
A program may use at most 128 MiB of HBM per device.

```python
import math
import jax
import jax.numpy as jnp
from jax import lax

DEPTH_STRATA = 8
HID = 128
ITERS = 3
FIN = 32
ZONAL_POINTS = 4096
MERIDIAN_POINTS = 2048


def columns_and_cells(key):
    regime_key, depth_key, open_key = jax.random.split(key, 3)
    basin_order = jax.random.permutation(regime_key, 12)
    deep_basin = (basin_order < 6).astype(jnp.int32).reshape(3, 4)
    lat_basin = jnp.arange(MERIDIAN_POINTS, dtype=jnp.int32) * 3 // MERIDIAN_POINTS
    lon_basin = jnp.arange(ZONAL_POINTS, dtype=jnp.int32) * 4 // ZONAL_POINTS
    deep_cells = deep_basin[lat_basin][:, lon_basin]
    column_levels = jax.random.randint(depth_key, (MERIDIAN_POINTS, ZONAL_POINTS), 0, 3).astype(jnp.int32)
    bottom = (column_levels + deep_cells * (DEPTH_STRATA - 2)).astype(jnp.int32)
    opened = jax.random.randint(open_key, (DEPTH_STRATA, MERIDIAN_POINTS, ZONAL_POINTS), 0, 10) > 0
    levels = jnp.arange(DEPTH_STRATA, dtype=jnp.int32)[:, None, None]
    sea_cells = jnp.logical_and(levels < bottom[None], opened).astype(jnp.int32)
    return (bottom, sea_cells)


def basin_strength(key, lower_log, upper_log):
    strength_key = jax.random.fold_in(key, 77)
    factor = jnp.exp(jax.random.uniform(strength_key, (4, 5), jnp.float32, lower_log, upper_log))
    lat_basin = jnp.arange(MERIDIAN_POINTS, dtype=jnp.int32) * 4 // MERIDIAN_POINTS
    lon_basin = jnp.arange(ZONAL_POINTS, dtype=jnp.int32) * 5 // ZONAL_POINTS
    return factor[lat_basin][:, lon_basin]


def current_field(base_key, strength):
    shape = (DEPTH_STRATA, MERIDIAN_POINTS, ZONAL_POINTS)
    values = jax.random.normal(base_key, shape, jnp.float32)
    return jnp.clip(values * strength[None], -6.0, 6.0)


def draw_sea_indicator_grid(key, part):
    bottom, sea_cells = columns_and_cells(key)
    return sea_cells


def draw_bathymetry_depth_index(key, part):
    bottom, sea_cells = columns_and_cells(key)
    return bottom


def draw_zonal_boundary_speed(key, part):
    base_key = jax.random.fold_in(key, 3)
    return current_field(base_key, basin_strength(key, -1.5, 1.0))


def draw_meridional_boundary_speed(key, part):
    base_key = jax.random.fold_in(key, 5)
    return current_field(base_key, basin_strength(key, -1.5, 1.0))


def steps_of(own_key, shape, shards, low, largest):
    loudness, own = 1.0, jax.random.fold_in(own_key, 6)
    for position, parts in shards:
        draws = jnp.exp(jax.random.uniform(jax.random.fold_in(own, position), (parts,), jnp.float32, low / len(shards), largest / len(shards)))
        loudness = loudness * jnp.repeat(draws, shape[position] // parts).reshape([-1 if axis == position else 1 for axis in range(len(shape))])
    return loudness


def normal_values(stream_key, extent, width, reach, pieces=(), kind=jnp.bfloat16):
    entries = width * jax.random.normal(stream_key, extent, jnp.float32)
    if pieces:
        entries = entries * steps_of(stream_key, extent, pieces, -0.22, 0.18)
    return jnp.clip(entries, -reach, reach).astype(kind)


def setup_inputs(seed: int = 0) -> dict:
    key_list = jax.random.split(jax.random.key(seed), 13)
    thermal_state = normal_values(key_list[0], (DEPTH_STRATA, MERIDIAN_POINTS, ZONAL_POINTS), 1.0, 6.0, ((1, 16), (2, 16)), jnp.float32)
    zonal_boundary_speed = draw_zonal_boundary_speed(jax.random.fold_in(key_list[12], 71), 0)
    meridional_boundary_speed = draw_meridional_boundary_speed(jax.random.fold_in(key_list[12], 71), 0)
    sea_indicator_grid = draw_sea_indicator_grid(jax.random.fold_in(key_list[12], 71), 0)
    bathymetry_depth_index = draw_bathymetry_depth_index(jax.random.fold_in(key_list[12], 71), 0)
    revised_thermal_adjoint = normal_values(key_list[5], (DEPTH_STRATA, MERIDIAN_POINTS, ZONAL_POINTS), 1.0, 6.0, ((1, 16), (2, 16)), jnp.float32)
    input_stratum_matrix = normal_values(key_list[6], (HID, FIN), FIN ** -0.5, 1.0, (), jnp.float32)
    input_stratum_offset = normal_values(key_list[7], (HID,), 0.5, 3.0, (), jnp.float32)
    hidden_stratum_matrix = normal_values(key_list[8], (HID, HID), HID ** -0.5, 0.5, (), jnp.float32)
    hidden_stratum_offset = normal_values(key_list[9], (HID,), 0.5, 3.0, (), jnp.float32)
    output_stratum_matrix = normal_values(key_list[10], (DEPTH_STRATA, HID), HID ** -0.5, 0.5, (), jnp.float32)
    output_stratum_offset = normal_values(key_list[11], (DEPTH_STRATA,), 1.0, 4.0, (), jnp.float32)
    return dict(thermal_state=thermal_state, zonal_boundary_speed=zonal_boundary_speed, meridional_boundary_speed=meridional_boundary_speed, sea_indicator_grid=sea_indicator_grid, bathymetry_depth_index=bathymetry_depth_index, revised_thermal_adjoint=revised_thermal_adjoint, input_stratum_matrix=input_stratum_matrix, input_stratum_offset=input_stratum_offset, hidden_stratum_matrix=hidden_stratum_matrix, hidden_stratum_offset=hidden_stratum_offset, output_stratum_matrix=output_stratum_matrix, output_stratum_offset=output_stratum_offset)


SIGMA = 0.5
PRESSURE_STEP = 1.0
TRANSPORT_TICK = 0.2
KAPPA_FLOOR = 0.02
KAPPA_SPAN = 0.4
GRADIENT_GAIN = 16.0

def east(field, shift=1):
    return jnp.roll(field, -shift, axis=-1)

def west(field):
    return jnp.roll(field, 1, axis=-1)

def north(field, shift=1):
    zeros = jnp.zeros(field.shape[:-2] + (shift, field.shape[-1]), field.dtype)
    return jnp.concatenate([field[..., shift:, :], zeros], axis=-2)

def south(field):
    zeros = jnp.zeros(field.shape[:-2] + (1, field.shape[-1]), field.dtype)
    return jnp.concatenate([zeros, field[..., :-1, :]], axis=-2)

def contract_columns(left, right):
    return lax.dot_general(left, right, (((1,), (1,)), ((), ())), preferred_element_type=jnp.float32)

def contract_rows(left, right):
    return lax.dot_general(left, right, (((0,), (0,)), ((), ())), preferred_element_type=jnp.float32)

def closure_block(features, pull, weights, biases):
    input_stratum_matrix, hidden_stratum_matrix, output_stratum_matrix = weights
    input_stratum_offset, hidden_stratum_offset, output_stratum_offset = biases
    first_value = jnp.tanh(jnp.dot(input_stratum_matrix, features, preferred_element_type=jnp.float32) + input_stratum_offset[:, None])
    first_stored = first_value.astype(jnp.bfloat16)
    second_value = jnp.tanh(jnp.dot(hidden_stratum_matrix, first_stored, preferred_element_type=jnp.float32) + hidden_stratum_offset[:, None])
    second_stored = second_value.astype(jnp.bfloat16)
    squash = jax.nn.sigmoid(jnp.dot(output_stratum_matrix, second_stored, preferred_element_type=jnp.float32) + output_stratum_offset[:, None])
    kappa = KAPPA_FLOOR + KAPPA_SPAN * squash
    outer_term = pull * KAPPA_SPAN * squash * (1.0 - squash)
    outer_grad = outer_term.astype(jnp.bfloat16)
    hidden_term = contract_rows(output_stratum_matrix, outer_grad) * (1.0 - second_value * second_value)
    hidden_grad = hidden_term.astype(jnp.bfloat16)
    inner_term = contract_rows(hidden_stratum_matrix, hidden_grad) * (1.0 - first_value * first_value)
    inner_grad = inner_term.astype(jnp.bfloat16)
    sums = (contract_columns(inner_grad, features), lax.optimization_barrier(jnp.sum(inner_term, axis=1)), contract_columns(hidden_grad, first_stored), lax.optimization_barrier(jnp.sum(hidden_term, axis=1)), contract_columns(outer_grad, second_stored), lax.optimization_barrier(jnp.sum(outer_term, axis=1)))
    return (kappa, sums)

def closure_field(features, pull, weights, biases, sum_shapes):
    feature_rows, meridian_strips, profile_points = features.shape
    populated_strata = pull.shape[0]
    strip_rows = 16

    def turn(index, carry):
        kappa, cumulative_sums_list = carry
        start = (index * strip_rows).astype(jnp.int32)
        block_features = lax.dynamic_slice_in_dim(features, start, strip_rows, 1).reshape(feature_rows, strip_rows * profile_points)
        block_pull = lax.dynamic_slice_in_dim(pull, start, strip_rows, 1).reshape(populated_strata, strip_rows * profile_points)
        block_kappa, block_sums = closure_block(block_features, block_pull, weights, biases)
        kappa = lax.dynamic_update_slice_in_dim(kappa, block_kappa.reshape(populated_strata, strip_rows, profile_points), start, 1)
        return (kappa, jax.tree.map(jnp.add, cumulative_sums_list, block_sums))
    initial = (jnp.zeros(pull.shape, jnp.float32), tuple((jnp.zeros(array_dimensions, jnp.float32) for array_dimensions in sum_shapes)))
    return lax.fori_loop(0, meridian_strips // strip_rows, turn, initial)

def reference(thermal_state, zonal_boundary_speed, meridional_boundary_speed, sea_indicator_grid, bathymetry_depth_index, revised_thermal_adjoint, input_stratum_matrix, input_stratum_offset, hidden_stratum_matrix, hidden_stratum_offset, output_stratum_matrix, output_stratum_offset):
    sea_indicator = sea_indicator_grid.astype(jnp.float32)
    scalar_quantity = thermal_state * sea_indicator
    depth = bathymetry_depth_index.astype(jnp.float32)
    east_wet = sea_indicator * east(sea_indicator)
    north_wet = sea_indicator * north(sea_indicator)
    east_depth = jnp.minimum(depth, east(depth))
    north_depth = jnp.minimum(depth, north(depth))
    east_transport = lax.optimization_barrier(jnp.sum(east_wet * zonal_boundary_speed, axis=0))
    north_transport = lax.optimization_barrier(jnp.sum(north_wet * meridional_boundary_speed, axis=0))
    source = -(east_transport - west(east_transport) + north_transport - south(north_transport))

    def operate(field):
        return SIGMA * field + east_depth * (field - east(field)) + west(east_depth) * (field - west(field)) + north_depth * (field - north(field)) + south(north_depth) * (field - south(field))
    sea_height_anomaly = jnp.zeros_like(source)
    residual = source
    direction = source
    norm_now = jnp.sum(residual * residual)
    for step in range(ITERS):
        image = operate(direction)
        alpha = norm_now / jnp.sum(direction * image)
        sea_height_anomaly = sea_height_anomaly + alpha * direction
        residual = residual - alpha * image
        norm_next = jnp.sum(residual * residual)
        direction = residual + norm_next / norm_now * direction
        norm_now = norm_next
    zonal_fixed = zonal_boundary_speed - PRESSURE_STEP * (east(sea_height_anomaly) - sea_height_anomaly)
    meridional_fixed = meridional_boundary_speed - PRESSURE_STEP * (north(sea_height_anomaly) - sea_height_anomaly)
    east_face = (7.0 * (scalar_quantity + east(scalar_quantity)) - (west(scalar_quantity) + east(scalar_quantity, 2))) / 12.0
    north_face = (7.0 * (scalar_quantity + north(scalar_quantity)) - (south(scalar_quantity) + north(scalar_quantity, 2))) / 12.0
    east_flux = east_wet * zonal_fixed * east_face
    north_flux = north_wet * meridional_fixed * north_face
    carry_scalar_downstream = -(east_flux - west(east_flux) + north_flux - south(north_flux))
    zonal_slope = 0.5 * (east(scalar_quantity) - west(scalar_quantity))
    meridional_slope = 0.5 * (north(scalar_quantity) - south(scalar_quantity))
    levels = jnp.arange(DEPTH_STRATA, dtype=jnp.float32)[:, None, None]
    clearance = sea_indicator * (depth[None] - levels) / DEPTH_STRATA
    features = jnp.concatenate([scalar_quantity, zonal_slope, meridional_slope, clearance], axis=0).astype(jnp.bfloat16)
    sea_indicator_couple = sea_indicator[:-1] * sea_indicator[1:]
    depth_stride_amount = scalar_quantity[1:] - scalar_quantity[:-1]
    zero_level = jnp.zeros_like(scalar_quantity[:1])
    neighbour_connection = sea_indicator_couple * (revised_thermal_adjoint[:-1] - revised_thermal_adjoint[1:]) * depth_stride_amount
    pull = 0.5 * (jnp.concatenate([neighbour_connection, zero_level], axis=0) + jnp.concatenate([zero_level, neighbour_connection], axis=0))
    weights = (input_stratum_matrix.astype(jnp.bfloat16), hidden_stratum_matrix.astype(jnp.bfloat16), output_stratum_matrix.astype(jnp.bfloat16))
    biases = (input_stratum_offset, hidden_stratum_offset, output_stratum_offset)
    sum_shapes = (input_stratum_matrix.shape, input_stratum_offset.shape, hidden_stratum_matrix.shape, hidden_stratum_offset.shape, output_stratum_matrix.shape, output_stratum_offset.shape)
    kappa, cumulative_sums_list = closure_field(features, pull, weights, biases, sum_shapes)
    down = 0.5 * (kappa[:-1] + kappa[1:]) * sea_indicator_couple * depth_stride_amount
    downward_mixing_operator = jnp.concatenate([down, zero_level], axis=0) - jnp.concatenate([zero_level, down], axis=0)
    revised_thermal_state = sea_indicator * (scalar_quantity + TRANSPORT_TICK * carry_scalar_downstream + downward_mixing_operator)
    multiplier_amount = GRADIENT_GAIN / math.sqrt(MERIDIAN_POINTS * ZONAL_POINTS)
    return (revised_thermal_state, sea_height_anomaly, cumulative_sums_list[0] * multiplier_amount, cumulative_sums_list[1] * multiplier_amount, cumulative_sums_list[2] * multiplier_amount, cumulative_sums_list[3] * multiplier_amount, cumulative_sums_list[4] * multiplier_amount, cumulative_sums_list[5] * multiplier_amount)
```

```python
import functools
import math

import jax
import jax.numpy as jnp
from jax import lax
from jax.experimental import pallas as pl
from jax.experimental.pallas import tpu as pltpu
from jax.sharding import PartitionSpec as P

LEVELS = 8
HID = 128
FIN = 32
ROWS = 128
COLS = 256
EXT_ROWS = ROWS + 16
EXT_COLS = COLS + 128
BLOCKS = ROWS // 8

SIGMA = 0.5
TRANSPORT_TICK = 0.2
KAPPA_FLOOR = 0.02
KAPPA_SPAN = 0.4
GRADIENT_GAIN = 16.0

CENTRE = 32.5
HALF_WIDTH = 32.0

TRACER_LANE, TRACER_WIDE = 0, 2
ZONAL_LANE, MERIDIAN_LANE, WET_LANE, DEPTH_LANE, WIDE = 16, 48, 80, 112, 4

ROW_INNER = 128
ROW_OUTER = 160
ROW_OUTER_BIAS = 168
ROW_BIAS = 176
ROW_GRAM = 184
SUM_ROWS = 256

F32 = jnp.float32
BF16 = jnp.bfloat16
VMEM_LIMIT = 48 * 1024 * 1024


def iota(shape, axis):
    return lax.broadcasted_iota(jnp.int32, shape, axis)


def turn(value, shift, axis):
    shift %= value.shape[axis]
    return pltpu.roll(value, shift, axis) if shift else value


def east(value):
    return turn(value, -1, value.ndim - 1)


def west(value):
    return turn(value, 1, value.ndim - 1)


def north(value):
    return turn(value, -1, value.ndim - 2)


def south(value):
    return turn(value, 1, value.ndim - 2)


def dot(left, right):
    return lax.dot_general(left, right, (((1,), (0,)), ((), ())), preferred_element_type=F32)


def dot_nt(left, right):
    return lax.dot_general(left, right, (((1,), (1,)), ((), ())), preferred_element_type=F32)


def pack_kernel(thermal, zonal, meridian, sea, depth, to_east, to_west, to_north, to_south):
    lane = iota((ROWS, 128), 1)
    low = iota((8, COLS), 0) < 4
    high_edge = jnp.zeros((ROWS, 128), F32)
    low_edge = jnp.zeros((ROWS, 128), F32)

    def place(edges, field, lane_start, wide):
        high, low_ = edges
        mask = jnp.logical_and(lane >= lane_start, lane < lane_start + wide)
        high = jnp.where(mask, turn(field[:, 128:], lane_start + wide, 1), high)
        low_ = jnp.where(mask, turn(field[:, :128], lane_start, 1), low_)
        return high, low_

    edges = (high_edge, low_edge)
    for k in range(LEVELS):
        wet = sea[k].astype(F32)
        tracer = thermal[k] * wet
        u = zonal[k]
        v = meridian[k]
        edges = place(edges, tracer, TRACER_LANE + TRACER_WIDE * k, TRACER_WIDE)
        edges = place(edges, u, ZONAL_LANE + WIDE * k, WIDE)
        edges = place(edges, v, MERIDIAN_LANE + WIDE * k, WIDE)
        edges = place(edges, wet, WET_LANE + WIDE * k, WIDE)
        to_north[k] = jnp.where(low, turn(v[ROWS - 8 :], 4, 0), tracer[ROWS - 8 :])
        to_north[LEVELS + k] = jnp.where(low, turn(wet[ROWS - 8 :], 4, 0), u[ROWS - 8 :])
        to_south[k] = jnp.where(low, tracer[:8], turn(v[:8], 4, 0))
        to_south[LEVELS + k] = jnp.where(low, u[:8], turn(wet[:8], 4, 0))
    floor = depth[...].astype(F32)
    edges = place(edges, floor, DEPTH_LANE, WIDE)
    to_north[2 * LEVELS] = floor[ROWS - 8 :]
    to_south[2 * LEVELS] = floor[:8]
    to_east[...] = edges[0]
    to_west[...] = edges[1]


def rows_extended(inside, south_tile, north_tile, second):
    if second:
        south_tile = turn(south_tile, 4, 0)
        north_tile = turn(north_tile, 4, 0)
    return jnp.concatenate([south_tile, inside, north_tile], axis=0)


def edge_columns(west_tile, east_tile, lane_start, wide):
    ahead = turn(east_tile, -lane_start, 1)
    behind = turn(west_tile, -wide - lane_start, 1)
    return jnp.where(iota(ahead.shape, 1) < 64, ahead, behind)


def closure_kernel(
    thermal, sea, depth, adjoint, south_edge, north_edge, west_edge, east_edge,
    w1, b1, w2, b2, w3, b3,
    base, sums,
    tracer_ext, tracer_cols, w1_big, w2_t, w3_big, w3_t, b1_wide, b2_wide,
    first, left, right, second, outer, slope1, slope2, grad, grad_outer, bias1, bias2, bias3,
):
    for k in range(LEVELS):
        tracer_ext[k, 0:8] = south_edge[k]
        tracer_ext[k, 8 : ROWS + 8] = thermal[k] * sea[k].astype(F32)
        tracer_ext[k, ROWS + 8 :] = north_edge[k]
        tracer_cols[k] = edge_columns(
            west_edge[...], east_edge[...], TRACER_LANE + TRACER_WIDE * k, TRACER_WIDE
        )
    inner_weight = w1[...].astype(BF16)
    hidden_weight = w2[...].astype(BF16)
    outer_weight = w3[...].astype(BF16)
    spread = (iota((FIN, 8 * FIN), 1) // 8 == iota((FIN, 8 * FIN), 0)).astype(BF16)
    inner_wide = dot(inner_weight, spread)
    inner_lane = iota((HID + FIN, 8 * FIN), 1)
    inner_row = iota((HID + FIN, 8 * FIN), 0) - HID
    stacked = jnp.concatenate([inner_wide, (inner_lane[HID:] // 8 == inner_row[HID:]).astype(F32)], 0)
    spread3 = (iota((LEVELS, 64), 1) // 8 == iota((LEVELS, 64), 0)).astype(BF16)
    outer_tall = lax.dot_general(
        spread3, outer_weight, (((0,), (0,)), ((), ())), preferred_element_type=F32
    )
    outer_wide = lax.dot_general(
        outer_weight, spread3, (((0,), (0,)), ((), ())), preferred_element_type=F32
    )
    pick_lane = iota((16, 64), 1)
    pick = (pick_lane // 8 == iota((16, 64), 0)).astype(F32)
    stacked3 = jnp.concatenate([outer_wide, pick], 0)
    lane3 = iota((HID + 16, 64), 1)
    row3 = iota((64, HID), 0)
    for r in range(8):
        w1_big[r] = jnp.where(inner_lane % 8 == r, stacked, 0.0).astype(BF16)
        w3_t[r] = jnp.where(lane3 % 8 == r, stacked3, 0.0).astype(BF16)
        w3_big[:, r * HID : (r + 1) * HID] = jnp.where(row3 % 8 == r, outer_tall, 0.0).astype(BF16)
    w2_t[...] = w2[...].T.astype(BF16)
    b1_wide[...] = jnp.broadcast_to(b1[...], (HID, COLS))
    b2_wide[...] = jnp.broadcast_to(b2[...], (HID, COLS))
    grad[...] = jnp.zeros_like(grad)
    grad_outer[...] = jnp.zeros_like(grad_outer)
    bias1[...] = jnp.zeros_like(bias1)
    bias2[...] = jnp.zeros_like(bias2)
    bias3[...] = jnp.zeros_like(bias3)
    level = iota((LEVELS, 8, COLS), 0).astype(F32)
    b3_cube = b3[...]

    def step(j, carry):
        start = pl.multiple_of(j * 8, 8)
        tall = tracer_ext[:, pl.ds(start, 24), :]
        tracer = tall[:, 8:16]
        wet = sea[:, pl.ds(start, 8), :].astype(F32)
        floor = depth[pl.ds(start, 8), :].astype(F32)
        wide = jnp.concatenate([tracer, tracer_cols[:, pl.ds(start, 8), :]], axis=2)
        zonal_slope = 0.5 * (east(wide)[:, :, :COLS] - west(wide)[:, :, :COLS])
        meridian_slope = 0.5 * (north(tall)[:, 8:16] - south(tall)[:, 8:16])
        clearance = wet * (floor[None] - level) * (1.0 / LEVELS)
        features = (
            jnp.concatenate([tracer, zonal_slope, meridian_slope, clearance], axis=0)
            .reshape(8 * FIN, COLS)
            .astype(BF16)
        )
        for r in range(8):
            z = dot(w1_big[r], features)
            value = jnp.tanh(z[:HID] + b1_wide[...])
            right[r, HID:] = value.astype(BF16)
            slope1[r] = 1.0 - value * value
            left[r, HID:] = z[HID:].astype(BF16)
        for r in range(8):
            value = jnp.tanh(dot(hidden_weight, right[r, HID:]) + b2_wide[...])
            second[r] = value.astype(BF16)
            slope2[r] = 1.0 - value * value
        squash = jax.nn.sigmoid(
            dot(w3_big[...], second[...].reshape(8 * HID, COLS)).reshape(LEVELS, 8, COLS) + b3_cube
        )
        kappa = KAPPA_FLOOR + KAPPA_SPAN * squash
        jump = tracer[1:] - tracer[:-1]
        pair_jump = wet[:-1] * wet[1:] * jump
        adj = adjoint[:, pl.ds(start, 8), :]
        bond = pair_jump * (adj[:-1] - adj[1:])
        none = jnp.zeros((1, 8, COLS), F32)
        pull = 0.5 * (jnp.concatenate([bond, none], 0) + jnp.concatenate([none, bond], 0))
        down = 0.5 * (kappa[:-1] + kappa[1:]) * pair_jump
        mixing = jnp.concatenate([down, none], 0) - jnp.concatenate([none, down], 0)
        base[:, pl.ds(start, 8), :] = wet * (tracer + mixing)
        outer_term = pull * KAPPA_SPAN * squash * (1.0 - squash)
        bias3[...] += outer_term
        outer_grad = outer_term.reshape(64, COLS).astype(BF16)
        total = grad[...]
        total_outer = grad_outer[...]
        total1 = bias1[...]
        total2 = bias2[...]
        for r in range(8):
            back = dot(w3_t[r], outer_grad)
            hidden_term = back[:HID] * slope2[r]
            total2 = total2 + hidden_term
            hidden_grad = hidden_term.astype(BF16)
            left[r, :HID] = hidden_grad
            outer[r] = back[HID:].astype(BF16)
            inner_term = dot(w2_t[...], hidden_grad) * slope1[r]
            total1 = total1 + inner_term
            right[r, :HID] = inner_term.astype(BF16)
            total = total + dot_nt(left[r], right[r])
            total_outer = total_outer + dot_nt(outer[r], second[r])
        grad[...] = total
        grad_outer[...] = total_outer
        bias1[...] = total1
        bias2[...] = total2
        return carry

    lax.fori_loop(0, BLOCKS, step, 0)
    sums[0:HID] = grad[0:HID, HID:]
    sums[ROW_INNER : ROW_INNER + FIN] = grad[HID:, :HID]
    sums[ROW_OUTER : ROW_OUTER + LEVELS] = grad_outer[0:LEVELS]
    outer_bias = jnp.sum(bias3[...], axis=1)
    sums[ROW_OUTER_BIAS : ROW_OUTER_BIAS + LEVELS] = outer_bias[:, :128] + outer_bias[:, 128:]
    inner_row_sum = jnp.sum((bias1[:, :128] + bias1[:, 128:]).T, axis=0, keepdims=True)
    hidden_row_sum = jnp.sum((bias2[:, :128] + bias2[:, 128:]).T, axis=0, keepdims=True)
    sums[ROW_BIAS : ROW_BIAS + 8] = jnp.concatenate(
        [inner_row_sum, hidden_row_sum, jnp.zeros((6, 128), F32)], 0
    )


def field_extended(inside, south_tile, north_tile, second, west_tile, east_tile, lane_start, wide):
    tall = rows_extended(inside, south_tile, north_tile, second)
    return jnp.concatenate([tall, edge_columns(west_tile, east_tile, lane_start, wide)], axis=1)


def gram_kernel(
    zonal, meridian, sea, depth, south_edge, north_edge, west_edge, east_edge,
    south_corner, north_corner, sums,
    basis, summed,
):
    west_tile = jnp.concatenate([south_corner[:, :128], west_edge[...], north_corner[:, :128]], 0)
    east_tile = jnp.concatenate([south_corner[:, 128:], east_edge[...], north_corner[:, 128:]], 0)

    def extended(inside, index, second, lane_start):
        return field_extended(
            inside, south_edge[index], north_edge[index], second, west_tile, east_tile, lane_start, WIDE
        )

    east_transport = jnp.zeros((EXT_ROWS, EXT_COLS), F32)
    north_transport = jnp.zeros((EXT_ROWS, EXT_COLS), F32)
    for k in range(LEVELS):
        wet = extended(sea[k].astype(F32), LEVELS + k, True, WET_LANE + WIDE * k)
        east_transport = east_transport + wet * east(wet) * extended(
            zonal[k], LEVELS + k, False, ZONAL_LANE + WIDE * k
        )
        north_transport = north_transport + wet * north(wet) * extended(
            meridian[k], k, True, MERIDIAN_LANE + WIDE * k
        )
    source = -(
        (east_transport - west(east_transport)) + (north_transport - south(north_transport))
    )
    floor = extended(depth[...].astype(F32), 2 * LEVELS, False, DEPTH_LANE)
    east_depth = jnp.minimum(floor, east(floor))
    north_depth = jnp.minimum(floor, north(floor))
    west_depth = west(east_depth)
    south_depth = south(north_depth)

    def operate(field):
        return (
            SIGMA * field
            + east_depth * (field - east(field))
            + west_depth * (field - west(field))
            + north_depth * (field - north(field))
            + south_depth * (field - south(field))
        )

    image0 = operate(source)
    first = (image0 - CENTRE * source) * (1.0 / HALF_WIDTH)
    image1 = operate(first)
    second = (image1 - CENTRE * first) * (2.0 / HALF_WIDTH) - source
    image2 = operate(second)
    basis[0] = source
    basis[1] = first
    basis[2] = second

    def product(a, b):
        inside = jnp.sum(a[8 : ROWS + 8, :COLS] * b[8 : ROWS + 8, :COLS], axis=0, keepdims=True)
        return inside[:, :128] + inside[:, 128:]

    rows = [
        product(source, image0),
        product(first, image0),
        product(second, image0),
        product(first, image1),
        product(second, image1),
        product(second, image2),
        product(source, source),
        product(first, source),
        product(second, source),
    ]
    summed[0:ROW_GRAM] = sums[0:ROW_GRAM]
    summed[ROW_GRAM : ROW_GRAM + 16] = jnp.concatenate(rows + [jnp.zeros((7, 128), F32)], 0)
    summed[ROW_GRAM + 16 :] = jnp.zeros((SUM_ROWS - ROW_GRAM - 16, 128), F32)


def galerkin(h00, h01, h02, h11, h12, h22, g0, g1, g2):
    tiny = 1e-6

    def pivot(value, scale):
        good = value > tiny * scale
        return jnp.where(good, 1.0 / jnp.where(good, value, 1.0), 0.0)

    p0 = pivot(h00, 0.0)
    l10 = h01 * p0
    l20 = h02 * p0
    d1 = h11 - l10 * h01
    p1 = pivot(d1, h11)
    s21 = h12 - l20 * h01
    l21 = s21 * p1
    d2 = h22 - l20 * h02 - l21 * s21
    p2 = pivot(d2, h22)
    z0 = g0
    z1 = g1 - l10 * z0
    z2 = g2 - l20 * z0 - l21 * z1
    y2 = z2 * p2
    y1 = z1 * p1 - l21 * y2
    y0 = z0 * p0 - l10 * y1 - l20 * y2
    return y0, y1, y2


def final_kernel(
    scale, thermal, zonal, meridian, sea, base, south_edge, north_edge, west_edge, east_edge, basis, totals,
    revised, height_out, grad1, bias1, grad2, bias2, grad3, bias3,
):
    gram = jnp.sum(totals[ROW_GRAM : ROW_GRAM + 16], axis=1, keepdims=True)
    y0, y1, y2 = galerkin(*[gram[i : i + 1] for i in range(9)])
    height = y0 * basis[0] + y1 * basis[1] + y2 * basis[2]
    height_out[...] = height[8 : ROWS + 8, :COLS]
    east_fall = east(height) - height
    north_fall = north(height) - height
    blank = jnp.zeros((8, 128), F32)
    west_tile = jnp.concatenate([blank, west_edge[...], blank], 0)
    east_tile = jnp.concatenate([blank, east_edge[...], blank], 0)
    for k in range(LEVELS):
        inside_wet = sea[k].astype(F32)
        wet = field_extended(
            inside_wet, south_edge[LEVELS + k], north_edge[LEVELS + k], True,
            west_tile, east_tile, WET_LANE + WIDE * k, WIDE,
        )
        tracer = field_extended(
            thermal[k] * inside_wet, south_edge[k], north_edge[k], False,
            west_tile, east_tile, TRACER_LANE + TRACER_WIDE * k, TRACER_WIDE,
        )
        u = jnp.concatenate(
            [zonal[k], edge_columns(west_edge[...], east_edge[...], ZONAL_LANE + WIDE * k, WIDE)], 1
        )
        v = rows_extended(meridian[k], south_edge[k], north_edge[k], True)
        mid_wet = wet[8 : ROWS + 8]
        mid = tracer[8 : ROWS + 8]
        pair = mid + east(mid)
        face = (8.0 * pair - (west(pair) + east(pair))) * (1.0 / 12.0)
        flux = mid_wet * east(mid_wet) * (u - east_fall[8 : ROWS + 8]) * face
        spread = (flux - west(flux))[:, :COLS]
        mid_wet = wet[:, :COLS]
        mid = tracer[:, :COLS]
        pair = mid + north(mid)
        face = (8.0 * pair - (south(pair) + north(pair))) * (1.0 / 12.0)
        flux = mid_wet * north(mid_wet) * (v - north_fall[:, :COLS]) * face
        spread = spread + (flux - south(flux))[8 : ROWS + 8]
        revised[k] = base[k] - TRANSPORT_TICK * (inside_wet * spread)
    grad2[...] = totals[0:HID] * scale
    grad1[...] = (totals[ROW_INNER : ROW_INNER + FIN] * scale).T
    grad3[...] = totals[ROW_OUTER : ROW_OUTER + LEVELS] * scale
    bias1[...] = totals[ROW_BIAS : ROW_BIAS + 1] * scale
    bias2[...] = totals[ROW_BIAS + 1 : ROW_BIAS + 2] * scale
    bias3[...] = jnp.sum(totals[ROW_OUTER_BIAS : ROW_OUTER_BIAS + LEVELS], axis=1, keepdims=True) * scale


def struct(*shape, dtype=F32):
    return jax.ShapeDtypeStruct(shape, dtype)


def call(kernel, out_shape, scratch=(), flops=0, transcendentals=0, nbytes=0):
    return pl.pallas_call(
        kernel,
        out_shape=out_shape,
        scratch_shapes=list(scratch),
        compiler_params=pltpu.CompilerParams(vmem_limit_bytes=VMEM_LIMIT),
        cost_estimate=pl.CostEstimate(
            flops=flops, transcendentals=transcendentals, bytes_accessed=nbytes
        ),
    )


def share(value, axis):
    count = lax.axis_size(axis)
    copies = jnp.broadcast_to(value[None], (count,) + value.shape)
    return jnp.sum(lax.all_to_all(copies, axis, 0, 0), axis=0)


def total_over_devices(value):
    count = lax.axis_size("lon")
    parts = value.reshape(count, value.shape[0] // count, value.shape[1])
    part = jnp.sum(lax.all_to_all(parts, "lon", 0, 0), axis=0)
    part = share(part, "lat")
    copies = jnp.broadcast_to(part[None], (count,) + part.shape)
    return lax.all_to_all(copies, "lon", 0, 0).reshape(value.shape)


def local(thermal, zonal, meridian, sea, depth, adjoint, w1, b1, w2, b2, w3, b3):
    lons, lats = lax.axis_size("lon"), lax.axis_size("lat")
    ring = [(i, (i + 1) % lons) for i in range(lons)]
    line = [(i, i + 1) for i in range(lats - 1)]

    def back(pairs):
        return [(target, source) for source, target in pairs]

    to_east, to_west, to_north, to_south = call(
        pack_kernel,
        (struct(ROWS, 128), struct(ROWS, 128), struct(17, 8, COLS), struct(17, 8, COLS)),
        flops=4_000_000,
        nbytes=5_000_000,
    )(thermal, zonal, meridian, sea, depth)
    west_edge = lax.ppermute(to_east, "lon", ring)
    east_edge = lax.ppermute(to_west, "lon", back(ring))
    south_edge = lax.ppermute(to_north, "lat", line)
    north_edge = lax.ppermute(to_south, "lat", back(line))
    edges = jnp.concatenate([west_edge, east_edge], axis=1)
    south_corner = lax.ppermute(edges[ROWS - 8 :], "lat", line)
    north_corner = lax.ppermute(edges[:8], "lat", back(line))

    base, sums = call(
        closure_kernel,
        (struct(LEVELS, ROWS, COLS), struct(ROW_GRAM, 128)),
        scratch=[
            pltpu.VMEM((LEVELS, EXT_ROWS, COLS), F32),
            pltpu.VMEM((LEVELS, ROWS, 128), F32),
            pltpu.VMEM((8, HID + FIN, 8 * FIN), BF16),
            pltpu.VMEM((HID, HID), BF16),
            pltpu.VMEM((64, 8 * HID), BF16),
            pltpu.VMEM((8, HID + 16, 64), BF16),
            pltpu.VMEM((HID, COLS), F32),
            pltpu.VMEM((HID, COLS), F32),
            pltpu.VMEM((8, HID, COLS), BF16),
            pltpu.VMEM((8, HID + FIN, COLS), BF16),
            pltpu.VMEM((8, 2 * HID, COLS), BF16),
            pltpu.VMEM((8, HID, COLS), BF16),
            pltpu.VMEM((8, 16, COLS), BF16),
            pltpu.VMEM((8, HID, COLS), F32),
            pltpu.VMEM((8, HID, COLS), F32),
            pltpu.VMEM((HID + FIN, COLS), F32),
            pltpu.VMEM((16, HID), F32),
            pltpu.VMEM((HID, COLS), F32),
            pltpu.VMEM((HID, COLS), F32),
            pltpu.VMEM((LEVELS, 8, COLS), F32),
        ],
        flops=8_000_000_000,
        transcendentals=9_000_000,
        nbytes=5_000_000,
    )(
        thermal, sea, depth, adjoint, south_edge, north_edge, west_edge, east_edge,
        w1, b1[:, None], w2, b2[:, None], w3, jnp.broadcast_to(b3[:, None, None], (LEVELS, 8, COLS)),
    )
    basis, summed = call(
        gram_kernel,
        (struct(3, EXT_ROWS, EXT_COLS), struct(SUM_ROWS, 128)),
        flops=20_000_000,
        nbytes=5_000_000,
    )(
        zonal, meridian, sea, depth, south_edge, north_edge, west_edge, east_edge,
        south_corner, north_corner, sums,
    )
    totals = total_over_devices(summed)
    scale = GRADIENT_GAIN / math.sqrt(ROWS * lats * COLS * lons)
    out = call(
        functools.partial(final_kernel, scale),
        (
            struct(LEVELS, ROWS, COLS),
            struct(ROWS, COLS),
            struct(HID, FIN),
            struct(1, HID),
            struct(HID, HID),
            struct(1, HID),
            struct(LEVELS, HID),
            struct(LEVELS, 1),
        ),
        flops=20_000_000,
        nbytes=8_000_000,
    )(
        thermal, zonal, meridian, sea, base, south_edge, north_edge, west_edge, east_edge, basis, totals
    )
    revised, height, grad1, bias1, grad2, bias2, grad3, bias3 = out
    return (
        revised,
        height,
        grad1,
        bias1.reshape(HID),
        grad2,
        bias2.reshape(HID),
        grad3,
        bias3.reshape(LEVELS),
    )


def solution(mesh):
    cube, plane, whole = P(None, "lat", "lon"), P("lat", "lon"), P()
    return jax.shard_map(
        local,
        mesh=mesh,
        in_specs=(cube, cube, cube, cube, plane, cube) + (whole,) * 6,
        out_specs=(cube, plane) + (whole,) * 6,
        check_vma=False,
    )
```

```python
import functools
import math

import jax
import jax.numpy as jnp
from jax import lax
from jax.experimental import pallas as pl
from jax.experimental.pallas import tpu as pltpu
from jax.sharding import PartitionSpec as P

LEVELS = 8
HID = 128
FIN = 32
ROWS = 128
COLS = 256
EXT_ROWS = ROWS + 16
EXT_COLS = COLS + 128
BLOCKS = ROWS // 8

SIGMA = 0.5
TRANSPORT_TICK = 0.2
KAPPA_FLOOR = 0.02
KAPPA_SPAN = 0.4
GRADIENT_GAIN = 16.0

CENTRE = 32.5
HALF_WIDTH = 32.0

TRACER_LANE, TRACER_WIDE = 0, 2
ZONAL_LANE, MERIDIAN_LANE, WET_LANE, DEPTH_LANE, WIDE = 16, 48, 80, 112, 4

ROW_INNER = 128
ROW_OUTER = 160
ROW_OUTER_BIAS = 168
ROW_BIAS = 176
ROW_GRAM = 184
SUM_ROWS = 256

F32 = jnp.float32
BF16 = jnp.bfloat16


def iota(shape, axis):
    return lax.broadcasted_iota(jnp.int32, shape, axis)


def turn(value, shift, axis):
    if isinstance(shift, int):
        shift %= value.shape[axis]
        return pltpu.roll(value, shift, axis) if shift else value
    return pltpu.roll(value, lax.rem(shift + value.shape[axis], value.shape[axis]), axis)


def east(value):
    return turn(value, -1, value.ndim - 1)


def west(value):
    return turn(value, 1, value.ndim - 1)


def north(value):
    return turn(value, -1, value.ndim - 2)


def south(value):
    return turn(value, 1, value.ndim - 2)


def dot(left, right):
    return lax.dot_general(left, right, (((1,), (0,)), ((), ())), preferred_element_type=F32)


def dot_nt(left, right):
    return lax.dot_general(left, right, (((1,), (1,)), ((), ())), preferred_element_type=F32)


def pack_kernel(
    thermal_far, zonal_far, meridian_far, sea_far, depth_far,
    to_east, to_west, to_north, to_south,
    thermal, zonal, meridian, sea, depth, arrived,
):
    fields = ((thermal_far, thermal), (zonal_far, zonal), (meridian_far, meridian), (sea_far, sea))
    depth_copy = pltpu.make_async_copy(depth_far, depth, arrived.at[4 * LEVELS])
    copies = []
    for k in range(LEVELS):
        copies.append(
            [
                pltpu.make_async_copy(far.at[k], near.at[k], arrived.at[4 * k + i])
                for i, (far, near) in enumerate(fields)
            ]
        )
        for copy in copies[k]:
            copy.start()
    depth_copy.start()
    lane = iota((ROWS, 128), 1)
    low = iota((8, COLS), 0) < 4
    high_edge = jnp.zeros((ROWS, 128), F32)
    low_edge = jnp.zeros((ROWS, 128), F32)

    def place(edges, field, lane_start, wide):
        high, low_ = edges
        mask = jnp.logical_and(lane >= lane_start, lane < lane_start + wide)
        high = jnp.where(mask, turn(field[:, 128:], lane_start + wide, 1), high)
        low_ = jnp.where(mask, turn(field[:, :128], lane_start, 1), low_)
        return high, low_

    edges = (high_edge, low_edge)
    for k in range(LEVELS):
        for copy in copies[k]:
            copy.wait()
        wet = sea[k].astype(F32)
        tracer = thermal[k] * wet
        u = zonal[k]
        v = meridian[k]
        edges = place(edges, tracer, TRACER_LANE + TRACER_WIDE * k, TRACER_WIDE)
        edges = place(edges, u, ZONAL_LANE + WIDE * k, WIDE)
        edges = place(edges, v, MERIDIAN_LANE + WIDE * k, WIDE)
        edges = place(edges, wet, WET_LANE + WIDE * k, WIDE)
        to_north[k] = jnp.where(low, turn(v[ROWS - 8 :], 4, 0), tracer[ROWS - 8 :])
        to_north[LEVELS + k] = jnp.where(low, turn(wet[ROWS - 8 :], 4, 0), u[ROWS - 8 :])
        to_south[k] = jnp.where(low, tracer[:8], turn(v[:8], 4, 0))
        to_south[LEVELS + k] = jnp.where(low, u[:8], turn(wet[:8], 4, 0))
    depth_copy.wait()
    floor = depth[...].astype(F32)
    edges = place(edges, floor, DEPTH_LANE, WIDE)
    to_north[2 * LEVELS] = floor[ROWS - 8 :]
    to_south[2 * LEVELS] = floor[:8]
    to_east[...] = edges[0]
    to_west[...] = edges[1]


def rows_extended(inside, south_tile, north_tile, second):
    if second:
        south_tile = turn(south_tile, 4, 0)
        north_tile = turn(north_tile, 4, 0)
    return jnp.concatenate([south_tile, inside, north_tile], axis=0)


def edge_columns(west_tile, east_tile, lane_start, wide):
    ahead = turn(east_tile, -lane_start, 1)
    behind = turn(west_tile, 128 - wide - lane_start, 1)
    return jnp.where(iota(ahead.shape, 1) < 64, ahead, behind)


def closure_kernel(
    thermal, sea, depth, adjoint, south_edge, north_edge, west_edge, east_edge,
    w1, b1, w2, b2, w3, b3,
    base, sums,
    tracer_ext, tracer_cols, w1_big, w2_pair, w2_pair_t, w3_big, w3_t, b1_wide, b2_wide,
    first0, left0, second0, slope10, slope20, outer0,
    first1, left1, second1, slope11, slope21, outer1,
    grad, grad_outer, bias1, bias2, bias3,
):
    for k in range(LEVELS):
        tracer_ext[k, 0:8] = south_edge[k]
        tracer_ext[k, 8 : ROWS + 8] = thermal[k] * sea[k].astype(F32)
        tracer_ext[k, ROWS + 8 :] = north_edge[k]
        tracer_cols[k] = edge_columns(
            west_edge[...], east_edge[...], TRACER_LANE + TRACER_WIDE * k, TRACER_WIDE
        )
    hidden_weight = w2[...].astype(BF16)
    outer_weight = w3[...].astype(BF16)
    spread = (iota((FIN, 8 * FIN), 1) // 8 == iota((FIN, 8 * FIN), 0)).astype(BF16)
    inner_wide = lax.dot_general(
        w1[...].astype(BF16), spread, (((0,), (0,)), ((), ())), preferred_element_type=F32
    )
    lane1 = iota((HID, 8 * FIN), 1)
    feature_lane = iota((FIN, 8 * FIN), 1) - 8 * iota((FIN, 8 * FIN), 0)
    spread3 = (iota((LEVELS, 64), 1) // 8 == iota((LEVELS, 64), 0)).astype(BF16)
    outer_tall = lax.dot_general(
        spread3, outer_weight, (((0,), (0,)), ((), ())), preferred_element_type=F32
    )
    outer_wide = lax.dot_general(
        outer_weight, spread3, (((0,), (0,)), ((), ())), preferred_element_type=F32
    )
    lane3 = iota((HID, 64), 1)
    row3 = iota((64, HID), 0)
    for r in range(8):
        w1_big[r * (HID + FIN) : r * (HID + FIN) + HID] = jnp.where(
            lane1 % 8 == r, inner_wide, 0.0
        ).astype(BF16)
        w1_big[r * (HID + FIN) + HID : (r + 1) * (HID + FIN)] = (feature_lane == r).astype(BF16)
        w3_t[r * HID : (r + 1) * HID] = jnp.where(lane3 % 8 == r, outer_wide, 0.0).astype(BF16)
        w3_big[:, r * HID : (r + 1) * HID] = jnp.where(row3 % 8 == r, outer_tall, 0.0).astype(BF16)
    blank = jnp.zeros((HID, HID), BF16)
    flipped = w2[...].T.astype(BF16)
    w2_pair[...] = jnp.concatenate(
        [jnp.concatenate([hidden_weight, blank], 1), jnp.concatenate([blank, hidden_weight], 1)], 0
    )
    w2_pair_t[...] = jnp.concatenate(
        [jnp.concatenate([flipped, blank], 1), jnp.concatenate([blank, flipped], 1)], 0
    )
    for bias, wide_bias in ((b1, b1_wide), (b2, b2_wide)):
        tall_bias = jnp.broadcast_to(bias[...], (HID, HID)).T
        wide_bias[...] = jnp.concatenate([tall_bias, tall_bias], 1)
    grad[...] = jnp.zeros_like(grad)
    grad_outer[...] = jnp.zeros_like(grad_outer)
    bias1[...] = jnp.zeros_like(bias1)
    bias2[...] = jnp.zeros_like(bias2)
    bias3[...] = jnp.zeros_like(bias3)
    level = iota((LEVELS, 8, COLS), 0).astype(F32)
    b3_cube = jnp.concatenate([jnp.full((1, 8, COLS), b3[k], F32) for k in range(LEVELS)], 0)

    def forward(j, first, left, second, slope1, slope2, outer):
        start = pl.multiple_of(j * 8, 8)
        tall = tracer_ext[:, pl.ds(start, 24), :]
        tracer = tall[:, 8:16]
        wet = sea[:, pl.ds(start, 8), :].astype(F32)
        floor = depth[pl.ds(start, 8), :].astype(F32)
        wide = jnp.concatenate([tracer, tracer_cols[:, pl.ds(start, 8), :]], axis=2)
        zonal_slope = 0.5 * (east(wide)[:, :, :COLS] - west(wide)[:, :, :COLS])
        meridian_slope = 0.5 * (north(tall)[:, 8:16] - south(tall)[:, 8:16])
        clearance = wet * (floor[None] - level) * (1.0 / LEVELS)
        features = (
            jnp.concatenate([tracer, zonal_slope, meridian_slope, clearance], axis=0)
            .reshape(8 * FIN, COLS)
            .astype(BF16)
        )
        yield
        for p in range(4):
            z = dot(w1_big[p * 2 * (HID + FIN) : (p + 1) * 2 * (HID + FIN)], features)
            for q in range(2):
                r = 2 * p + q
                z0 = q * (HID + FIN)
                value = jnp.tanh(z[z0 : z0 + HID] + b1_wide[...])
                first[r * HID : (r + 1) * HID] = value.astype(BF16)
                slope1[r] = 1.0 - value * value
                left[r, HID:] = z[z0 + HID : z0 + HID + FIN].astype(BF16)
            yield
        for p in range(4):
            z = dot(w2_pair[...], first[p * 2 * HID : (p + 1) * 2 * HID])
            for q in range(2):
                r = 2 * p + q
                value = jnp.tanh(z[q * HID : (q + 1) * HID] + b2_wide[...])
                second[r * HID : (r + 1) * HID] = value.astype(BF16)
                slope2[r] = 1.0 - value * value
            yield
        squash = jax.nn.sigmoid(
            dot(w3_big[...], second[...]).reshape(LEVELS, 8, COLS) + b3_cube
        )
        kappa = KAPPA_FLOOR + KAPPA_SPAN * squash
        jump = tracer[1:] - tracer[:-1]
        pair_jump = wet[:-1] * wet[1:] * jump
        adj = adjoint[:, pl.ds(start, 8), :]
        bond = pair_jump * (adj[:-1] - adj[1:])
        none = jnp.zeros((1, 8, COLS), F32)
        pull = 0.5 * (jnp.concatenate([bond, none], 0) + jnp.concatenate([none, bond], 0))
        down = 0.5 * (kappa[:-1] + kappa[1:]) * pair_jump
        mixing = jnp.concatenate([down, none], 0) - jnp.concatenate([none, down], 0)
        base[:, pl.ds(start, 8), :] = wet * (tracer + mixing)
        outer[...] = pull * KAPPA_SPAN * squash * (1.0 - squash)

    def backward(first, left, second, slope1, slope2, outer):
        outer_term = outer[...]
        bias3[...] += outer_term
        outer_grad = outer_term.reshape(64, COLS).astype(BF16)
        total1 = bias1[...]
        total2 = bias2[...]
        terms = []
        for p in range(4):
            back = dot(w3_t[p * 2 * HID : (p + 1) * 2 * HID], outer_grad)
            for q in range(2):
                r = 2 * p + q
                hidden_term = back[q * HID : (q + 1) * HID] * slope2[r]
                total2 = total2 + hidden_term
                left[r, :HID] = hidden_term.astype(BF16)
            yield
        bias2[...] = total2
        total = grad[...]
        for p in range(4):
            z = dot(w2_pair_t[...], jnp.concatenate([left[2 * p, :HID], left[2 * p + 1, :HID]], 0))
            for q in range(2):
                r = 2 * p + q
                inner_term = z[q * HID : (q + 1) * HID] * slope1[r]
                total1 = total1 + inner_term
                right = jnp.concatenate(
                    [inner_term.astype(BF16), first[r * HID : (r + 1) * HID]], 0
                )
                total = total + dot_nt(left[r], right)
            yield
        bias1[...] = total1
        grad[...] = total
        grad_outer[...] += dot_nt(outer_grad, second[...])

    def together(*parts):
        parts = list(parts)
        while parts:
            for part in list(parts):
                if next(part, parts) is parts:
                    parts.remove(part)

    even = (first0, left0, second0, slope10, slope20, outer0)
    odd = (first1, left1, second1, slope11, slope21, outer1)
    together(forward(0, *even))

    def step(i, carry):
        together(forward(2 * i + 1, *odd), backward(*even))
        together(forward(jnp.minimum(2 * i + 2, BLOCKS - 1), *even), backward(*odd))
        return carry

    lax.fori_loop(0, BLOCKS // 2, step, 0)
    sums[0:HID] = grad[0:HID, HID:]
    sums[ROW_INNER : ROW_INNER + FIN] = grad[HID:, :HID]
    row_outer = iota((64, HID), 0)
    outer_sum = jnp.zeros((64, HID), F32)
    for r in range(8):
        outer_sum = outer_sum + jnp.where(
            row_outer % 8 == r, grad_outer[:, r * HID : (r + 1) * HID], 0.0
        )
    sums[ROW_OUTER : ROW_OUTER + LEVELS] = jnp.sum(outer_sum.reshape(LEVELS, 8, HID), axis=1)
    outer_bias = jnp.sum(bias3[...], axis=1)
    sums[ROW_OUTER_BIAS : ROW_OUTER_BIAS + LEVELS] = outer_bias[:, :128] + outer_bias[:, 128:]
    inner_row_sum = jnp.sum((bias1[:, :128] + bias1[:, 128:]).T, axis=0, keepdims=True)
    hidden_row_sum = jnp.sum((bias2[:, :128] + bias2[:, 128:]).T, axis=0, keepdims=True)
    sums[ROW_BIAS : ROW_BIAS + 8] = jnp.concatenate(
        [inner_row_sum, hidden_row_sum, jnp.zeros((6, 128), F32)], 0
    )


def field_extended(inside, south_tile, north_tile, second, west_tile, east_tile, lane_start, wide):
    tall = rows_extended(inside, south_tile, north_tile, second)
    return jnp.concatenate([tall, edge_columns(west_tile, east_tile, lane_start, wide)], axis=1)


def gram_kernel(
    zonal, meridian, sea, depth, south_edge, north_edge, west_edge, east_edge,
    south_corner, north_corner, sums,
    basis, summed,
    east_transport, north_transport,
):
    west_tile = jnp.concatenate([south_corner[:, :128], west_edge[...], north_corner[:, :128]], 0)
    east_tile = jnp.concatenate([south_corner[:, 128:], east_edge[...], north_corner[:, 128:]], 0)

    def extended(inside, index, second, lane_start):
        return field_extended(
            inside, south_edge[index], north_edge[index], second, west_tile, east_tile, lane_start, WIDE
        )

    def gather(k, carry):
        wet = extended(sea[k].astype(F32), LEVELS + k, True, WET_LANE + WIDE * k)
        east_part = wet * east(wet) * extended(
            zonal[k], LEVELS + k, False, ZONAL_LANE + WIDE * k
        )
        north_part = wet * north(wet) * extended(
            meridian[k], k, True, MERIDIAN_LANE + WIDE * k
        )
        east_transport[...] += east_part
        north_transport[...] += north_part
        return carry

    east_transport[...] = jnp.zeros_like(east_transport)
    north_transport[...] = jnp.zeros_like(north_transport)
    lax.fori_loop(0, LEVELS, gather, 0)
    source = -(
        (east_transport[...] - west(east_transport[...]))
        + (north_transport[...] - south(north_transport[...]))
    )
    floor = extended(depth[...].astype(F32), 2 * LEVELS, False, DEPTH_LANE)
    east_depth = jnp.minimum(floor, east(floor))
    north_depth = jnp.minimum(floor, north(floor))
    west_depth = west(east_depth)
    south_depth = south(north_depth)

    def operate(field):
        return (
            SIGMA * field
            + east_depth * (field - east(field))
            + west_depth * (field - west(field))
            + north_depth * (field - north(field))
            + south_depth * (field - south(field))
        )

    image0 = operate(source)
    first = (image0 - CENTRE * source) * (1.0 / HALF_WIDTH)
    image1 = operate(first)
    second = (image1 - CENTRE * first) * (2.0 / HALF_WIDTH) - source
    image2 = operate(second)
    basis[0] = source
    basis[1] = first
    basis[2] = second

    def product(a, b):
        inside = jnp.sum(a[8 : ROWS + 8, :COLS] * b[8 : ROWS + 8, :COLS], axis=0, keepdims=True)
        return inside[:, :128] + inside[:, 128:]

    rows = [
        product(source, image0),
        product(first, image0),
        product(second, image0),
        product(first, image1),
        product(second, image1),
        product(second, image2),
        product(source, source),
        product(first, source),
        product(second, source),
    ]
    summed[0:ROW_GRAM] = sums[0:ROW_GRAM]
    summed[ROW_GRAM : ROW_GRAM + 16] = jnp.concatenate(rows + [jnp.zeros((7, 128), F32)], 0)
    summed[ROW_GRAM + 16 :] = jnp.zeros((SUM_ROWS - ROW_GRAM - 16, 128), F32)


def galerkin(h00, h01, h02, h11, h12, h22, g0, g1, g2):
    tiny = 1e-6

    def pivot(value, scale):
        good = value > tiny * scale
        return jnp.where(good, 1.0 / jnp.where(good, value, 1.0), 0.0)

    p0 = pivot(h00, 0.0)
    l10 = h01 * p0
    l20 = h02 * p0
    d1 = h11 - l10 * h01
    p1 = pivot(d1, h11)
    s21 = h12 - l20 * h01
    l21 = s21 * p1
    d2 = h22 - l20 * h02 - l21 * s21
    p2 = pivot(d2, h22)
    z0 = g0
    z1 = g1 - l10 * z0
    z2 = g2 - l20 * z0 - l21 * z1
    y2 = z2 * p2
    y1 = z1 * p1 - l21 * y2
    y0 = z0 * p0 - l10 * y1 - l20 * y2
    return y0, y1, y2


def final_kernel(
    scale, thermal, zonal, meridian, sea, base, south_edge, north_edge, west_edge, east_edge, basis, totals,
    revised, height_out, grad1, bias1, grad2, bias2, grad3, bias3,
    falls,
):
    gram = jnp.sum(totals[ROW_GRAM : ROW_GRAM + 16], axis=1, keepdims=True)
    y0, y1, y2 = galerkin(*[gram[i : i + 1] for i in range(9)])
    height = y0 * basis[0] + y1 * basis[1] + y2 * basis[2]
    height_out[...] = height[8 : ROWS + 8, :COLS]
    blank = jnp.zeros((8, 128), F32)
    west_tile = jnp.concatenate([blank, west_edge[...], blank], 0)
    east_tile = jnp.concatenate([blank, east_edge[...], blank], 0)
    falls[0] = east(height) - height
    falls[1] = north(height) - height
    def advect(k, carry):
        inside_wet = sea[k].astype(F32)
        wet = field_extended(
            inside_wet, south_edge[LEVELS + k], north_edge[LEVELS + k], True,
            west_tile, east_tile, WET_LANE + WIDE * k, WIDE,
        )
        tracer = field_extended(
            thermal[k] * inside_wet, south_edge[k], north_edge[k], False,
            west_tile, east_tile, TRACER_LANE + TRACER_WIDE * k, TRACER_WIDE,
        )
        u = jnp.concatenate(
            [zonal[k], edge_columns(west_edge[...], east_edge[...], ZONAL_LANE + WIDE * k, WIDE)], 1
        )
        v = rows_extended(meridian[k], south_edge[k], north_edge[k], True)
        mid_wet = wet[8 : ROWS + 8]
        mid = tracer[8 : ROWS + 8]
        pair = mid + east(mid)
        face = (8.0 * pair - (west(pair) + east(pair))) * (1.0 / 12.0)
        flux = mid_wet * east(mid_wet) * (u - falls[0, 8 : ROWS + 8]) * face
        spread = (flux - west(flux))[:, :COLS]
        mid_wet = wet[:, :COLS]
        mid = tracer[:, :COLS]
        pair = mid + north(mid)
        face = (8.0 * pair - (south(pair) + north(pair))) * (1.0 / 12.0)
        flux = mid_wet * north(mid_wet) * (v - falls[1, :, :COLS]) * face
        spread = spread + (flux - south(flux))[8 : ROWS + 8]
        revised[k] = base[k] - TRANSPORT_TICK * (inside_wet * spread)
        return carry

    lax.fori_loop(0, LEVELS, advect, 0)
    grad2[...] = totals[0:HID] * scale
    grad1[...] = totals[ROW_INNER : ROW_INNER + FIN] * scale
    grad3[...] = totals[ROW_OUTER : ROW_OUTER + LEVELS] * scale
    bias1[...] = totals[ROW_BIAS : ROW_BIAS + 1] * scale
    bias2[...] = totals[ROW_BIAS + 1 : ROW_BIAS + 2] * scale
    outer_bias = jnp.sum(totals[ROW_OUTER_BIAS : ROW_OUTER_BIAS + LEVELS], axis=1, keepdims=True)
    diagonal = iota((LEVELS, LEVELS), 0) == iota((LEVELS, LEVELS), 1)
    bias3[...] = jnp.sum(jnp.where(diagonal, outer_bias * scale, 0.0), axis=0, keepdims=True)


def struct(*shape, dtype=F32):
    return jax.ShapeDtypeStruct(shape, dtype)


def call(kernel, out_shape, scratch=(), in_specs=None, mib=16, flops=0, transcendentals=0, nbytes=0):
    specs = {} if in_specs is None else {"in_specs": in_specs}
    return pl.pallas_call(
        kernel,
        out_shape=out_shape,
        scratch_shapes=list(scratch),
        compiler_params=pltpu.CompilerParams(vmem_limit_bytes=mib * 1024 * 1024),
        cost_estimate=pl.CostEstimate(
            flops=flops, transcendentals=transcendentals, bytes_accessed=nbytes
        ),
        **specs,
    )


def near(count):
    return [pl.BlockSpec(memory_space=pltpu.VMEM)] * count


def far(count):
    return [pl.BlockSpec(memory_space=pltpu.HBM)] * count


def sum_kernel(parts, copies):
    total = parts[0]
    for i in range(1, parts.shape[0]):
        total = total + parts[i]
    for i in range(copies.shape[0]):
        copies[i] = total


def summed_copies(parts, count):
    return call(sum_kernel, struct(count, *parts.shape[1:]), mib=4, nbytes=300_000)(parts)


def total_over_devices(value):
    lons, lats = lax.axis_size("lon"), lax.axis_size("lat")
    parts = value.reshape(lons, value.shape[0] // lons, value.shape[1])
    parts = lax.all_to_all(parts, "lon", 0, 0)
    parts = lax.all_to_all(summed_copies(parts, lats), "lat", 0, 0)
    parts = lax.all_to_all(summed_copies(parts, lons), "lon", 0, 0)
    return parts.reshape(value.shape)


def local(thermal, zonal, meridian, sea, depth, adjoint, w1, b1, w2, b2, w3, b3):
    lons, lats = lax.axis_size("lon"), lax.axis_size("lat")
    ring = [(i, (i + 1) % lons) for i in range(lons)]
    line = [(i, i + 1) for i in range(lats - 1)]

    def back(pairs):
        return [(target, source) for source, target in pairs]

    to_east, to_west, to_north, to_south = call(
        pack_kernel,
        (struct(ROWS, 128), struct(ROWS, 128), struct(17, 8, COLS), struct(17, 8, COLS)),
        scratch=[
            pltpu.VMEM((LEVELS, ROWS, COLS), F32),
            pltpu.VMEM((LEVELS, ROWS, COLS), F32),
            pltpu.VMEM((LEVELS, ROWS, COLS), F32),
            pltpu.VMEM((LEVELS, ROWS, COLS), jnp.int32),
            pltpu.VMEM((ROWS, COLS), jnp.int32),
            pltpu.SemaphoreType.DMA((4 * LEVELS + 1,)),
        ],
        in_specs=far(5),
        mib=58,
        flops=4_000_000,
        nbytes=5_000_000,
    )(thermal, zonal, meridian, sea, depth)
    west_edge = lax.ppermute(to_east, "lon", ring)
    east_edge = lax.ppermute(to_west, "lon", back(ring))
    south_edge = lax.ppermute(to_north, "lat", line)
    north_edge = lax.ppermute(to_south, "lat", back(line))
    edges = jnp.concatenate([west_edge, east_edge], axis=1)
    south_corner = lax.ppermute(edges[ROWS - 8 :], "lat", line)
    north_corner = lax.ppermute(edges[:8], "lat", back(line))

    base, sums = call(
        closure_kernel,
        (struct(LEVELS, ROWS, COLS), struct(ROW_GRAM, 128)),
        scratch=[
            pltpu.VMEM((LEVELS, EXT_ROWS, COLS), F32),
            pltpu.VMEM((LEVELS, ROWS, 128), F32),
            pltpu.VMEM((8 * (HID + FIN), 8 * FIN), BF16),
            pltpu.VMEM((2 * HID, 2 * HID), BF16),
            pltpu.VMEM((2 * HID, 2 * HID), BF16),
            pltpu.VMEM((64, 8 * HID), BF16),
            pltpu.VMEM((8 * HID, 64), BF16),
            pltpu.VMEM((HID, COLS), F32),
            pltpu.VMEM((HID, COLS), F32),
        ]
        + 2
        * [
            pltpu.VMEM((8 * HID, COLS), BF16),
            pltpu.VMEM((8, HID + FIN, COLS), BF16),
            pltpu.VMEM((8 * HID, COLS), BF16),
            pltpu.VMEM((8, HID, COLS), F32),
            pltpu.VMEM((8, HID, COLS), F32),
            pltpu.VMEM((LEVELS, 8, COLS), F32),
        ]
        + [
            pltpu.VMEM((HID + FIN, COLS), F32),
            pltpu.VMEM((64, 8 * HID), F32),
            pltpu.VMEM((HID, COLS), F32),
            pltpu.VMEM((HID, COLS), F32),
            pltpu.VMEM((LEVELS, 8, COLS), F32),
        ],
        in_specs=near(13) + [pl.BlockSpec(memory_space=pltpu.SMEM)],
        mib=24,
        flops=8_000_000_000,
        transcendentals=9_000_000,
        nbytes=5_000_000,
    )(
        thermal, sea, depth, adjoint, south_edge, north_edge, west_edge, east_edge,
        w1.T, b1[None], w2, b2[None], w3, b3,
    )
    basis, summed = call(
        gram_kernel,
        (struct(3, EXT_ROWS, EXT_COLS), struct(SUM_ROWS, 128)),
        scratch=[pltpu.VMEM((EXT_ROWS, EXT_COLS), F32)] * 2,
        flops=20_000_000,
        nbytes=5_000_000,
    )(
        zonal, meridian, sea, depth, south_edge, north_edge, west_edge, east_edge,
        south_corner, north_corner, sums,
    )
    totals = total_over_devices(summed)
    scale = GRADIENT_GAIN / math.sqrt(ROWS * lats * COLS * lons)
    out = call(
        functools.partial(final_kernel, scale),
        (
            struct(LEVELS, ROWS, COLS),
            struct(ROWS, COLS),
            struct(FIN, HID),
            struct(1, HID),
            struct(HID, HID),
            struct(1, HID),
            struct(LEVELS, HID),
            struct(1, LEVELS),
        ),
        scratch=[pltpu.VMEM((2, EXT_ROWS, EXT_COLS), F32)],
        flops=20_000_000,
        nbytes=8_000_000,
    )(
        thermal, zonal, meridian, sea, base, south_edge, north_edge, west_edge, east_edge, basis, totals
    )
    revised, height, grad1, bias1, grad2, bias2, grad3, bias3 = out
    return (
        revised,
        height,
        grad1.T,
        bias1.reshape(HID),
        grad2,
        bias2.reshape(HID),
        grad3,
        bias3.reshape(LEVELS),
    )


def solution(mesh):
    cube, plane, whole = P(None, "lat", "lon"), P("lat", "lon"), P()
    return jax.shard_map(
        local,
        mesh=mesh,
        in_specs=(cube, cube, cube, cube, plane, cube) + (whole,) * 6,
        out_specs=(cube, plane) + (whole,) * 6,
        check_vma=False,
    )
```

```python
import functools
import math

import jax
import jax.numpy as jnp
from jax import lax
from jax.experimental import pallas as pl
from jax.experimental.pallas import tpu as pltpu
from jax.sharding import PartitionSpec as P

LEVELS = 8
HID = 128
FIN = 32
ROWS = 128
COLS = 256
EXT_ROWS = ROWS + 16
EXT_COLS = COLS + 128
BLOCKS = ROWS // 8

SIGMA = 0.5
TRANSPORT_TICK = 0.2
KAPPA_FLOOR = 0.02
KAPPA_SPAN = 0.4
GRADIENT_GAIN = 16.0

CENTRE = 32.5
HALF_WIDTH = 32.0

TRACER_LANE, TRACER_WIDE = 0, 2
ZONAL_LANE, MERIDIAN_LANE, WET_LANE, DEPTH_LANE, WIDE = 16, 48, 80, 112, 4

ROW_INNER = 128
ROW_OUTER = 160
ROW_OUTER_BIAS = 168
ROW_BIAS = 176
SUM_ROWS = 192

F32 = jnp.float32
BF16 = jnp.bfloat16


def iota(shape, axis):
    return lax.broadcasted_iota(jnp.int32, shape, axis)


def turn(value, shift, axis):
    if isinstance(shift, int):
        shift %= value.shape[axis]
        return pltpu.roll(value, shift, axis) if shift else value
    return pltpu.roll(value, lax.rem(shift + value.shape[axis], value.shape[axis]), axis)


def east(value):
    return turn(value, -1, value.ndim - 1)


def west(value):
    return turn(value, 1, value.ndim - 1)


def north(value):
    return turn(value, -1, value.ndim - 2)


def south(value):
    return turn(value, 1, value.ndim - 2)


def dot(left, right):
    return lax.dot_general(left, right, (((1,), (0,)), ((), ())), preferred_element_type=F32)


def dot_nt(left, right):
    return lax.dot_general(left, right, (((1,), (1,)), ((), ())), preferred_element_type=F32)


def pack_rows_kernel(
    thermal_far, zonal_far, meridian_far, sea_far, depth_far,
    to_north, to_south,
    floats, seas, floors, arrived,
):
    copies = []
    for side, start in enumerate((ROWS - 8, 0)):
        rows = pl.ds(start, 8)
        pairs = [
            (thermal_far.at[:, rows], floats.at[3 * side]),
            (zonal_far.at[:, rows], floats.at[3 * side + 1]),
            (meridian_far.at[:, rows], floats.at[3 * side + 2]),
            (sea_far.at[:, rows], seas.at[side]),
            (depth_far.at[rows], floors.at[side]),
        ]
        copies += [
            pltpu.make_async_copy(source, target, arrived.at[5 * side + i])
            for i, (source, target) in enumerate(pairs)
        ]
    for copy in copies:
        copy.start()
    for copy in copies:
        copy.wait()
    low = iota((8, COLS), 0) < 4
    for k in range(LEVELS):
        wet = seas[0, k].astype(F32)
        to_north[k] = jnp.where(low, turn(floats[2, k], 4, 0), floats[0, k] * wet)
        to_north[LEVELS + k] = jnp.where(low, turn(wet, 4, 0), floats[1, k])
        wet = seas[1, k].astype(F32)
        to_south[k] = jnp.where(low, floats[3, k] * wet, turn(floats[5, k], 4, 0))
        to_south[LEVELS + k] = jnp.where(low, floats[4, k], turn(wet, 4, 0))
    to_north[2 * LEVELS] = floors[0].astype(F32)
    to_south[2 * LEVELS] = floors[1].astype(F32)


def place(edges, field, lane_start, wide):
    lane = iota((field.shape[0], 128), 1)
    mask = jnp.logical_and(lane >= lane_start, lane < lane_start + wide)
    high = jnp.where(mask, turn(field[:, 128:], lane_start + wide, 1), edges[0])
    low = jnp.where(mask, turn(field[:, :128], lane_start, 1), edges[1])
    return high, low


def place_level(edges, k, tracer, u, v, wet):
    edges = place(edges, tracer, TRACER_LANE + TRACER_WIDE * k, TRACER_WIDE)
    edges = place(edges, u, ZONAL_LANE + WIDE * k, WIDE)
    edges = place(edges, v, MERIDIAN_LANE + WIDE * k, WIDE)
    return place(edges, wet, WET_LANE + WIDE * k, WIDE)


def pack_columns_kernel(thermal, zonal, meridian, sea, depth, high, low):
    edges = (jnp.zeros((ROWS, 128), F32), jnp.zeros((ROWS, 128), F32))
    for k in range(LEVELS):
        wet = sea[k].astype(F32)
        edges = place_level(edges, k, thermal[k] * wet, zonal[k], meridian[k], wet)
    edges = place(edges, depth[...].astype(F32), DEPTH_LANE, WIDE)
    high[...], low[...] = edges


def pack_corners_kernel(south_edge, north_edge, to_east, to_west):
    for edge, start in ((south_edge, 0), (north_edge, 8)):
        edges = (jnp.zeros((8, 128), F32), jnp.zeros((8, 128), F32))
        for k in range(LEVELS):
            edges = place_level(
                edges, k, edge[k], edge[LEVELS + k], turn(edge[k], 4, 0), turn(edge[LEVELS + k], 4, 0)
            )
        edges = place(edges, edge[2 * LEVELS], DEPTH_LANE, WIDE)
        to_east[start : start + 8], to_west[start : start + 8] = edges


def with_corners(edge, corner):
    return jnp.concatenate([corner[:8], edge[...], corner[8:]], axis=0)


def rows_extended(inside, south_tile, north_tile, second):
    if second:
        south_tile = turn(south_tile, 4, 0)
        north_tile = turn(north_tile, 4, 0)
    return jnp.concatenate([south_tile, inside, north_tile], axis=0)


def edge_columns(west_tile, east_tile, lane_start, wide):
    ahead = turn(east_tile, -lane_start, 1)
    behind = turn(west_tile, 128 - wide - lane_start, 1)
    return jnp.where(iota(ahead.shape, 1) < 64, ahead, behind)


def closure_kernel(
    thermal, sea, depth, adjoint, south_edge, north_edge, west_edge, east_edge,
    w1, b1, w2, b2, w3, b3,
    base, sums,
    tracer_ext, tracer_cols, w1_big, w2_pair, w2_pair_t, w3_big, w3_t, b1_wide, b2_wide,
    first0, left0, second0, slope10, slope20, outer0,
    first1, left1, second1, slope11, slope21, outer1,
    grad, grad_outer, bias1, bias2, bias3,
):
    for k in range(LEVELS):
        tracer_ext[k, 0:8] = south_edge[k]
        tracer_ext[k, 8 : ROWS + 8] = thermal[k] * sea[k].astype(F32)
        tracer_ext[k, ROWS + 8 :] = north_edge[k]
        tracer_cols[k] = edge_columns(
            west_edge[...], east_edge[...], TRACER_LANE + TRACER_WIDE * k, TRACER_WIDE
        )
    hidden_weight = w2[...].astype(BF16)
    outer_weight = w3[...].astype(BF16)
    spread = (iota((FIN, 8 * FIN), 1) // 8 == iota((FIN, 8 * FIN), 0)).astype(BF16)
    inner_wide = lax.dot_general(
        w1[...].astype(BF16), spread, (((0,), (0,)), ((), ())), preferred_element_type=F32
    )
    lane1 = iota((HID, 8 * FIN), 1)
    feature_lane = iota((FIN, 8 * FIN), 1) - 8 * iota((FIN, 8 * FIN), 0)
    spread3 = (iota((LEVELS, 64), 1) // 8 == iota((LEVELS, 64), 0)).astype(BF16)
    outer_tall = lax.dot_general(
        spread3, outer_weight, (((0,), (0,)), ((), ())), preferred_element_type=F32
    )
    outer_wide = lax.dot_general(
        outer_weight, spread3, (((0,), (0,)), ((), ())), preferred_element_type=F32
    )
    lane3 = iota((HID, 64), 1)
    row3 = iota((64, HID), 0)
    for r in range(8):
        w1_big[r * (HID + FIN) : r * (HID + FIN) + HID] = jnp.where(
            lane1 % 8 == r, inner_wide, 0.0
        ).astype(BF16)
        w1_big[r * (HID + FIN) + HID : (r + 1) * (HID + FIN)] = (feature_lane == r).astype(BF16)
        w3_t[r * HID : (r + 1) * HID] = jnp.where(lane3 % 8 == r, outer_wide, 0.0).astype(BF16)
        w3_big[:, r * HID : (r + 1) * HID] = jnp.where(row3 % 8 == r, outer_tall, 0.0).astype(BF16)
    blank = jnp.zeros((HID, HID), BF16)
    flipped = w2[...].T.astype(BF16)
    w2_pair[...] = jnp.concatenate(
        [jnp.concatenate([hidden_weight, blank], 1), jnp.concatenate([blank, hidden_weight], 1)], 0
    )
    w2_pair_t[...] = jnp.concatenate(
        [jnp.concatenate([flipped, blank], 1), jnp.concatenate([blank, flipped], 1)], 0
    )
    for bias, wide_bias in ((b1, b1_wide), (b2, b2_wide)):
        tall_bias = jnp.broadcast_to(bias[...], (HID, HID)).T
        wide_bias[...] = jnp.concatenate([tall_bias, tall_bias], 1)
    grad[...] = jnp.zeros_like(grad)
    grad_outer[...] = jnp.zeros_like(grad_outer)
    bias1[...] = jnp.zeros_like(bias1)
    bias2[...] = jnp.zeros_like(bias2)
    bias3[...] = jnp.zeros_like(bias3)
    level = iota((LEVELS, 8, COLS), 0).astype(F32)
    b3_cube = jnp.concatenate([jnp.full((1, 8, COLS), b3[k], F32) for k in range(LEVELS)], 0)

    def forward(j, first, left, second, slope1, slope2, outer):
        start = pl.multiple_of(j * 8, 8)
        tall = tracer_ext[:, pl.ds(start, 24), :]
        tracer = tall[:, 8:16]
        wet = sea[:, pl.ds(start, 8), :].astype(F32)
        floor = depth[pl.ds(start, 8), :].astype(F32)
        wide = jnp.concatenate([tracer, tracer_cols[:, pl.ds(start, 8), :]], axis=2)
        zonal_slope = 0.5 * (east(wide)[:, :, :COLS] - west(wide)[:, :, :COLS])
        meridian_slope = 0.5 * (north(tall)[:, 8:16] - south(tall)[:, 8:16])
        clearance = wet * (floor[None] - level) * (1.0 / LEVELS)
        features = (
            jnp.concatenate([tracer, zonal_slope, meridian_slope, clearance], axis=0)
            .reshape(8 * FIN, COLS)
            .astype(BF16)
        )
        yield
        for p in range(4):
            z = dot(w1_big[p * 2 * (HID + FIN) : (p + 1) * 2 * (HID + FIN)], features)
            for q in range(2):
                r = 2 * p + q
                z0 = q * (HID + FIN)
                value = jnp.tanh(z[z0 : z0 + HID] + b1_wide[...])
                first[r * HID : (r + 1) * HID] = value.astype(BF16)
                slope1[r] = 1.0 - value * value
                left[r, HID:] = z[z0 + HID : z0 + HID + FIN].astype(BF16)
            yield
        for p in range(4):
            z = dot(w2_pair[...], first[p * 2 * HID : (p + 1) * 2 * HID])
            for q in range(2):
                r = 2 * p + q
                value = jnp.tanh(z[q * HID : (q + 1) * HID] + b2_wide[...])
                second[r * HID : (r + 1) * HID] = value.astype(BF16)
                slope2[r] = 1.0 - value * value
            yield
        squash = jax.nn.sigmoid(
            dot(w3_big[...], second[...]).reshape(LEVELS, 8, COLS) + b3_cube
        )
        kappa = KAPPA_FLOOR + KAPPA_SPAN * squash
        jump = tracer[1:] - tracer[:-1]
        pair_jump = wet[:-1] * wet[1:] * jump
        adj = adjoint[:, pl.ds(start, 8), :]
        bond = pair_jump * (adj[:-1] - adj[1:])
        none = jnp.zeros((1, 8, COLS), F32)
        pull = 0.5 * (jnp.concatenate([bond, none], 0) + jnp.concatenate([none, bond], 0))
        down = 0.5 * (kappa[:-1] + kappa[1:]) * pair_jump
        mixing = jnp.concatenate([down, none], 0) - jnp.concatenate([none, down], 0)
        base[:, pl.ds(start, 8), :] = tracer + mixing
        outer[...] = pull * KAPPA_SPAN * squash * (1.0 - squash)

    def backward(first, left, second, slope1, slope2, outer):
        outer_term = outer[...]
        bias3[...] += outer_term
        outer_grad = outer_term.reshape(64, COLS).astype(BF16)
        total1 = bias1[...]
        total2 = bias2[...]
        terms = []
        for p in range(4):
            back = dot(w3_t[p * 2 * HID : (p + 1) * 2 * HID], outer_grad)
            for q in range(2):
                r = 2 * p + q
                hidden_term = back[q * HID : (q + 1) * HID] * slope2[r]
                total2 = total2 + hidden_term
                left[r, :HID] = hidden_term.astype(BF16)
            cols = slice(p * 2 * HID, (p + 1) * 2 * HID)
            grad_outer[:, cols] += dot_nt(outer_grad, second[cols])
            yield
        bias2[...] = total2
        total = grad[...]
        rights = []
        for p in range(4):
            z = dot(w2_pair_t[...], jnp.concatenate([left[2 * p, :HID], left[2 * p + 1, :HID]], 0))
            for q in range(2):
                r = 2 * p + q
                inner_term = z[q * HID : (q + 1) * HID] * slope1[r]
                total1 = total1 + inner_term
                rights.append(jnp.concatenate(
                    [inner_term.astype(BF16), first[r * HID : (r + 1) * HID]], 0
                ))
            if p:
                for r in (2 * p - 2, 2 * p - 1):
                    total = total + dot_nt(left[r], rights[r])
            yield
        yield
        for r in (6, 7):
            total = total + dot_nt(left[r], rights[r])
        bias1[...] = total1
        grad[...] = total

    def together(*parts):
        parts = list(parts)
        while parts:
            for part in list(parts):
                if next(part, parts) is parts:
                    parts.remove(part)

    even = (first0, left0, second0, slope10, slope20, outer0)
    odd = (first1, left1, second1, slope11, slope21, outer1)
    together(forward(0, *even))

    def step(i, carry):
        together(forward(2 * i + 1, *odd), backward(*even))
        together(forward(jnp.minimum(2 * i + 2, BLOCKS - 1), *even), backward(*odd))
        return carry

    lax.fori_loop(0, BLOCKS // 2 - 1, step, 0)
    together(forward(BLOCKS - 1, *odd), backward(*even))
    together(backward(*odd))
    sums[0:HID] = grad[0:HID, HID:]
    sums[ROW_INNER : ROW_INNER + FIN] = grad[HID:, :HID]
    row_outer = iota((64, HID), 0)
    outer_sum = jnp.zeros((64, HID), F32)
    for r in range(8):
        outer_sum = outer_sum + jnp.where(
            row_outer % 8 == r, grad_outer[:, r * HID : (r + 1) * HID], 0.0
        )
    sums[ROW_OUTER : ROW_OUTER + LEVELS] = jnp.sum(outer_sum.reshape(LEVELS, 8, HID), axis=1)
    outer_bias = jnp.sum(bias3[...], axis=1)
    sums[ROW_OUTER_BIAS : ROW_OUTER_BIAS + LEVELS] = outer_bias[:, :128] + outer_bias[:, 128:]
    inner_row_sum = jnp.sum((bias1[:, :128] + bias1[:, 128:]).T, axis=0, keepdims=True)
    hidden_row_sum = jnp.sum((bias2[:, :128] + bias2[:, 128:]).T, axis=0, keepdims=True)
    sums[ROW_BIAS:] = jnp.concatenate(
        [inner_row_sum, hidden_row_sum, jnp.zeros((SUM_ROWS - ROW_BIAS - 2, 128), F32)], 0
    )


def field_extended(inside, south_tile, north_tile, second, west_tile, east_tile, lane_start, wide):
    tall = rows_extended(inside, south_tile, north_tile, second)
    return jnp.concatenate([tall, edge_columns(west_tile, east_tile, lane_start, wide)], axis=1)


def gram_kernel(
    zonal, meridian, sea, depth, south_edge, north_edge, west_edge, east_edge, west_corner, east_corner,
    sums,
    basis, parts, east_open, north_open,
    east_transport, north_transport, east_bits, north_bits,
):
    west_tile = with_corners(west_edge, west_corner)
    east_tile = with_corners(east_edge, east_corner)

    def extended(inside, index, second, lane_start):
        return field_extended(
            inside, south_edge[index], north_edge[index], second,
            west_tile, east_tile, lane_start, WIDE,
        )

    def gather(k, carry):
        wet = extended(sea[k].astype(F32), LEVELS + k, True, WET_LANE + WIDE * k)
        east_pair = wet * east(wet)
        north_pair = wet * north(wet)
        east_transport[...] += east_pair * extended(
            zonal[k], LEVELS + k, False, ZONAL_LANE + WIDE * k
        )
        north_transport[...] += north_pair * extended(
            meridian[k], k, True, MERIDIAN_LANE + WIDE * k
        )
        place_value = lax.shift_left(jnp.int32(1), k).astype(F32)
        east_bits[...] += east_pair[8 : ROWS + 8] * place_value
        north_bits[...] += north_pair[:, :COLS] * place_value
        return carry

    for total in (east_transport, north_transport, east_bits, north_bits):
        total[...] = jnp.zeros_like(total)
    lax.fori_loop(0, LEVELS, gather, 0)
    east_open[...] = east_bits[...].astype(jnp.int32)
    north_open[...] = north_bits[...].astype(jnp.int32)
    source = -(
        (east_transport[...] - west(east_transport[...]))
        + (north_transport[...] - south(north_transport[...]))
    )
    floor = extended(depth[...].astype(F32), 2 * LEVELS, False, DEPTH_LANE)
    east_depth = jnp.minimum(floor, east(floor))
    north_depth = jnp.minimum(floor, north(floor))
    west_depth = west(east_depth)
    south_depth = south(north_depth)

    def operate(field):
        return (
            SIGMA * field
            + east_depth * (field - east(field))
            + west_depth * (field - west(field))
            + north_depth * (field - north(field))
            + south_depth * (field - south(field))
        )

    image0 = operate(source)
    first = (image0 - CENTRE * source) * (1.0 / HALF_WIDTH)
    image1 = operate(first)
    second = (image1 - CENTRE * first) * (2.0 / HALF_WIDTH) - source
    image2 = operate(second)
    basis[0] = source
    basis[1] = first
    basis[2] = second

    lane = iota((1, 128), 1)
    gram = jnp.zeros((1, 128), F32)
    pairs = (
        (source, image0), (first, image0), (second, image0),
        (first, image1), (second, image1), (second, image2),
        (source, source), (first, source), (second, source),
    )
    for i, (a, b) in enumerate(pairs):
        total = jnp.sum(a[8 : ROWS + 8, :COLS] * b[8 : ROWS + 8, :COLS], axis=0, keepdims=True)
        gram = jnp.where(lane == i, jnp.sum(total, axis=1, keepdims=True), gram)
    count, tall, _ = parts.shape
    own = SUM_ROWS // count
    tail = jnp.broadcast_to(gram, (tall - own, 128))
    for i in range(count):
        parts[i, :own] = sums[i * own : (i + 1) * own]
        parts[i, own:] = tail


def galerkin(h00, h01, h02, h11, h12, h22, g0, g1, g2):
    tiny = 1e-6

    def pivot(value, scale):
        good = value > tiny * scale
        return jnp.where(good, 1.0 / jnp.where(good, value, 1.0), 0.0)

    p0 = pivot(h00, 0.0)
    l10 = h01 * p0
    l20 = h02 * p0
    d1 = h11 - l10 * h01
    p1 = pivot(d1, h11)
    s21 = h12 - l20 * h01
    l21 = s21 * p1
    d2 = h22 - l20 * h02 - l21 * s21
    p2 = pivot(d2, h22)
    z0 = g0
    z1 = g1 - l10 * z0
    z2 = g2 - l20 * z0 - l21 * z1
    y2 = z2 * p2
    y1 = z1 * p1 - l21 * y2
    y0 = z0 * p0 - l10 * y1 - l20 * y2
    return y0, y1, y2


def final_kernel(
    scale, thermal, zonal, meridian, sea, base, south_edge, north_edge, west_edge, east_edge,
    west_corner, east_corner, basis, east_open, north_open, parts,
    revised_far, height_out, grad1, bias1, grad2, bias2, grad3, bias3,
    revised, falls, west_tile, east_tile, totals, sent,
):
    def store(k):
        return pltpu.make_async_copy(revised.at[k], revised_far.at[k], sent.at[k])

    count = parts.shape[0]
    own = SUM_ROWS // count
    gram = parts[0, own : own + 1]
    y0, y1, y2 = galerkin(*[gram[:, i : i + 1] for i in range(9)])
    height = y0 * basis[0] + y1 * basis[1] + y2 * basis[2]
    height_out[...] = height[8 : ROWS + 8, :COLS]
    falls[0] = east(height) - height
    falls[1] = north(height) - height
    west_tile[...] = with_corners(west_edge, west_corner)
    east_tile[...] = with_corners(east_edge, east_corner)

    def level(k, carry):
        bit = lax.shift_left(jnp.int32(1), k)
        tracer = field_extended(
            thermal[k] * sea[k].astype(F32), south_edge[k], north_edge[k], False,
            west_tile[...], east_tile[...], TRACER_LANE + TRACER_WIDE * k, TRACER_WIDE,
        )
        u = jnp.concatenate([zonal[k], turn(west_edge[...], 128 - WIDE - ZONAL_LANE - WIDE * k, 1)], 1)
        v = rows_extended(meridian[k], south_edge[k], north_edge[k], True)
        mid = tracer[8 : ROWS + 8]
        pair = mid + east(mid)
        face = 8.0 * pair - (west(pair) + east(pair))
        flux = jnp.where((east_open[...] & bit) != 0, (u - falls[0, 8 : ROWS + 8]) * face, 0.0)
        spread = (flux - west(flux))[:, :COLS]
        mid = tracer[:, :COLS]
        pair = mid + north(mid)
        face = 8.0 * pair - (south(pair) + north(pair))
        flux = jnp.where((north_open[...] & bit) != 0, (v - falls[1, :, :COLS]) * face, 0.0)
        spread = spread + (flux - south(flux))[8 : ROWS + 8]
        revised[k] = base[k] - (TRANSPORT_TICK / 12.0) * spread
        store(k).start()
        return carry

    lax.fori_loop(0, LEVELS, level, 0)
    for i in range(count):
        totals[i * own : (i + 1) * own] = parts[i, :own] * scale
    grad2[...] = totals[0:HID]
    grad1[...] = totals[ROW_INNER : ROW_INNER + FIN]
    grad3[...] = totals[ROW_OUTER : ROW_OUTER + LEVELS]
    bias1[...] = totals[ROW_BIAS : ROW_BIAS + 1]
    bias2[...] = totals[ROW_BIAS + 1 : ROW_BIAS + 2]
    outer_bias = jnp.sum(totals[ROW_OUTER_BIAS : ROW_OUTER_BIAS + LEVELS], axis=1, keepdims=True)
    diagonal = iota((LEVELS, LEVELS), 0) == iota((LEVELS, LEVELS), 1)
    bias3[...] = jnp.sum(jnp.where(diagonal, outer_bias, 0.0), axis=0, keepdims=True)
    for k in range(LEVELS):
        store(k).wait()


def struct(*shape, dtype=F32):
    return jax.ShapeDtypeStruct(shape, dtype)


def call(kernel, out_shape, scratch=(), mib=16, flops=0, transcendentals=0, nbytes=0, **specs):
    return pl.pallas_call(
        kernel,
        out_shape=out_shape,
        scratch_shapes=list(scratch),
        compiler_params=pltpu.CompilerParams(vmem_limit_bytes=mib * 1024 * 1024),
        cost_estimate=pl.CostEstimate(
            flops=flops, transcendentals=transcendentals, bytes_accessed=nbytes
        ),
        **specs,
    )


def near(count):
    return [pl.BlockSpec(memory_space=pltpu.VMEM)] * count


def far(count):
    return [pl.BlockSpec(memory_space=pltpu.HBM)] * count


def sum_kernel(parts, copies):
    total = parts[0]
    for i in range(1, parts.shape[0]):
        total = total + parts[i]
    for i in range(copies.shape[0]):
        copies[i] = total


def summed_copies(parts, count):
    return call(sum_kernel, struct(count, *parts.shape[1:]), mib=4, nbytes=300_000)(parts)


def local(thermal, zonal, meridian, sea, depth, adjoint, w1, b1, w2, b2, w3, b3):
    lons, lats = lax.axis_size("lon"), lax.axis_size("lat")
    ring = [(i, (i + 1) % lons) for i in range(lons)]
    line = [(i, i + 1) for i in range(lats - 1)]

    def back(pairs):
        return [(target, source) for source, target in pairs]

    to_north, to_south = call(
        pack_rows_kernel,
        (struct(17, 8, COLS), struct(17, 8, COLS)),
        scratch=[
            pltpu.VMEM((6, LEVELS, 8, COLS), F32),
            pltpu.VMEM((2, LEVELS, 8, COLS), jnp.int32),
            pltpu.VMEM((2, 8, COLS), jnp.int32),
            pltpu.SemaphoreType.DMA((10,)),
        ],
        in_specs=far(5),
        mib=58,
        nbytes=1_000_000,
    )(thermal, zonal, meridian, sea, depth)
    south_edge = lax.ppermute(to_north, "lat", line)
    north_edge = lax.ppermute(to_south, "lat", back(line))
    high, low = call(
        pack_columns_kernel,
        (struct(ROWS, 128), struct(ROWS, 128)),
        mib=8,
        flops=4_000_000,
        nbytes=5_000_000,
    )(thermal, zonal, meridian, sea, depth)
    west_edge = lax.ppermute(high, "lon", ring)
    east_edge = lax.ppermute(low, "lon", back(ring))
    to_east, to_west = call(
        pack_corners_kernel,
        (struct(16, 128), struct(16, 128)),
        mib=4,
        nbytes=400_000,
    )(south_edge, north_edge)
    west_corner = lax.ppermute(to_east, "lon", ring)
    east_corner = lax.ppermute(to_west, "lon", back(ring))

    base, sums = call(
        closure_kernel,
        (struct(LEVELS, ROWS, COLS), struct(SUM_ROWS, 128)),
        scratch=[
            pltpu.VMEM((LEVELS, EXT_ROWS, COLS), F32),
            pltpu.VMEM((LEVELS, ROWS, 128), F32),
            pltpu.VMEM((8 * (HID + FIN), 8 * FIN), BF16),
            pltpu.VMEM((2 * HID, 2 * HID), BF16),
            pltpu.VMEM((2 * HID, 2 * HID), BF16),
            pltpu.VMEM((64, 8 * HID), BF16),
            pltpu.VMEM((8 * HID, 64), BF16),
            pltpu.VMEM((HID, COLS), F32),
            pltpu.VMEM((HID, COLS), F32),
        ]
        + 2
        * [
            pltpu.VMEM((8 * HID, COLS), BF16),
            pltpu.VMEM((8, HID + FIN, COLS), BF16),
            pltpu.VMEM((8 * HID, COLS), BF16),
            pltpu.VMEM((8, HID, COLS), F32),
            pltpu.VMEM((8, HID, COLS), F32),
            pltpu.VMEM((LEVELS, 8, COLS), F32),
        ]
        + [
            pltpu.VMEM((HID + FIN, COLS), F32),
            pltpu.VMEM((64, 8 * HID), F32),
            pltpu.VMEM((HID, COLS), F32),
            pltpu.VMEM((HID, COLS), F32),
            pltpu.VMEM((LEVELS, 8, COLS), F32),
        ],
        in_specs=near(13) + [pl.BlockSpec(memory_space=pltpu.SMEM)],
        mib=24,
        flops=8_000_000_000,
        transcendentals=9_000_000,
        nbytes=5_000_000,
    )(
        thermal, sea, depth, adjoint, south_edge, north_edge, west_edge, east_edge,
        w1.T, b1[None], w2, b2[None], w3, b3,
    )
    basis, parts, east_open, north_open = call(
        gram_kernel,
        (
            struct(3, EXT_ROWS, EXT_COLS),
            struct(lons, (SUM_ROWS // lons // 8 + 1) * 8, 128),
            struct(ROWS, EXT_COLS, dtype=jnp.int32),
            struct(EXT_ROWS, COLS, dtype=jnp.int32),
        ),
        scratch=[pltpu.VMEM((EXT_ROWS, EXT_COLS), F32)] * 2
        + [pltpu.VMEM((ROWS, EXT_COLS), F32), pltpu.VMEM((EXT_ROWS, COLS), F32)],
        flops=20_000_000,
        nbytes=5_000_000,
    )(
        zonal, meridian, sea, depth, south_edge, north_edge, west_edge, east_edge, west_corner, east_corner,
        sums,
    )
    parts = lax.all_to_all(parts, "lon", 0, 0)
    parts = lax.all_to_all(summed_copies(parts, lats), "lat", 0, 0)
    parts = lax.all_to_all(summed_copies(parts, lons), "lon", 0, 0)
    scale = GRADIENT_GAIN / math.sqrt(ROWS * lats * COLS * lons)
    revised, height, grad1, bias1, grad2, bias2, grad3, bias3 = call(
        functools.partial(final_kernel, scale),
        (
            struct(LEVELS, ROWS, COLS),
            struct(ROWS, COLS),
            struct(FIN, HID),
            struct(1, HID),
            struct(HID, HID),
            struct(1, HID),
            struct(LEVELS, HID),
            struct(1, LEVELS),
        ),
        scratch=[
            pltpu.VMEM((LEVELS, ROWS, COLS), F32),
            pltpu.VMEM((2, EXT_ROWS, EXT_COLS), F32),
            pltpu.VMEM((EXT_ROWS, 128), F32),
            pltpu.VMEM((EXT_ROWS, 128), F32),
            pltpu.VMEM((SUM_ROWS, 128), F32),
            pltpu.SemaphoreType.DMA((LEVELS,)),
        ],
        out_specs=tuple(far(1) + near(7)),
        flops=20_000_000,
        nbytes=8_000_000,
    )(
        thermal, zonal, meridian, sea, base, south_edge, north_edge, west_edge, east_edge,
        west_corner, east_corner, basis, east_open, north_open, parts,
    )
    return (
        revised,
        height,
        grad1.T,
        bias1.reshape(HID),
        grad2,
        bias2.reshape(HID),
        grad3,
        bias3.reshape(LEVELS),
    )


def solution(mesh):
    cube, plane, whole = P(None, "lat", "lon"), P("lat", "lon"), P()
    return jax.shard_map(
        local,
        mesh=mesh,
        in_specs=(cube, cube, cube, cube, plane, cube) + (whole,) * 6,
        out_specs=(cube, plane) + (whole,) * 6,
        check_vma=False,
    )
```

```python
import functools
import math

import jax
import jax.numpy as jnp
from jax import lax
from jax.experimental import pallas as pl
from jax.experimental.pallas import tpu as pltpu
from jax.sharding import PartitionSpec as P

LEVELS = 8
HID = 128
FIN = 32
ROWS = 128
COLS = 256
EXT_ROWS = ROWS + 16
EXT_COLS = COLS + 128
BLOCKS = ROWS // 8

SIGMA = 0.5
TRANSPORT_TICK = 0.2
KAPPA_FLOOR = 0.02
KAPPA_SPAN = 0.4
GRADIENT_GAIN = 16.0

CENTRE = 32.5
HALF_WIDTH = 32.0

TRACER_LANE, TRACER_WIDE = 0, 2
ZONAL_LANE, MERIDIAN_LANE, WET_LANE, DEPTH_LANE, WIDE = 16, 48, 80, 112, 4

ROW_INNER = 128
ROW_OUTER = 160
ROW_OUTER_BIAS = 168
ROW_BIAS = 176
SUM_ROWS = 192

F32 = jnp.float32
BF16 = jnp.bfloat16


def iota(shape, axis):
    return lax.broadcasted_iota(jnp.int32, shape, axis)


def turn(value, shift, axis):
    if isinstance(shift, int):
        shift %= value.shape[axis]
        return pltpu.roll(value, shift, axis) if shift else value
    return pltpu.roll(value, lax.rem(shift + value.shape[axis], value.shape[axis]), axis)


def east(value):
    return turn(value, -1, value.ndim - 1)


def west(value):
    return turn(value, 1, value.ndim - 1)


def north(value):
    return turn(value, -1, value.ndim - 2)


def south(value):
    return turn(value, 1, value.ndim - 2)


def dot(left, right):
    return lax.dot_general(left, right, (((1,), (0,)), ((), ())), preferred_element_type=F32)


def dot_nt(left, right):
    return lax.dot_general(left, right, (((1,), (1,)), ((), ())), preferred_element_type=F32)


def pack_rows_kernel(
    thermal_far, zonal_far, meridian_far, sea_far, depth_far,
    to_north, to_south,
    floats, seas, floors, arrived,
):
    copies = []
    for side, start in enumerate((ROWS - 8, 0)):
        rows = pl.ds(start, 8)
        pairs = [
            (thermal_far.at[:, rows], floats.at[3 * side]),
            (zonal_far.at[:, rows], floats.at[3 * side + 1]),
            (meridian_far.at[:, rows], floats.at[3 * side + 2]),
            (sea_far.at[:, rows], seas.at[side]),
            (depth_far.at[rows], floors.at[side]),
        ]
        copies += [
            pltpu.make_async_copy(source, target, arrived.at[5 * side + i])
            for i, (source, target) in enumerate(pairs)
        ]
    for copy in copies:
        copy.start()
    for copy in copies:
        copy.wait()
    low = iota((8, COLS), 0) < 4
    for k in range(LEVELS):
        wet = seas[0, k].astype(F32)
        to_north[k] = jnp.where(low, turn(floats[2, k], 4, 0), floats[0, k] * wet)
        to_north[LEVELS + k] = jnp.where(low, turn(wet, 4, 0), floats[1, k])
        wet = seas[1, k].astype(F32)
        to_south[k] = jnp.where(low, floats[3, k] * wet, turn(floats[5, k], 4, 0))
        to_south[LEVELS + k] = jnp.where(low, floats[4, k], turn(wet, 4, 0))
    to_north[2 * LEVELS] = floors[0].astype(F32)
    to_south[2 * LEVELS] = floors[1].astype(F32)


def place(edges, field, lane_start, wide):
    lane = iota((field.shape[0], 128), 1)
    mask = jnp.logical_and(lane >= lane_start, lane < lane_start + wide)
    high = jnp.where(mask, turn(field[:, 128:], lane_start + wide, 1), edges[0])
    low = jnp.where(mask, turn(field[:, :128], lane_start, 1), edges[1])
    return high, low


def place_level(edges, k, tracer, u, v, wet):
    edges = place(edges, tracer, TRACER_LANE + TRACER_WIDE * k, TRACER_WIDE)
    edges = place(edges, u, ZONAL_LANE + WIDE * k, WIDE)
    edges = place(edges, v, MERIDIAN_LANE + WIDE * k, WIDE)
    return place(edges, wet, WET_LANE + WIDE * k, WIDE)


def pack_columns_kernel(thermal, zonal, meridian, sea, depth, high, low):
    edges = (jnp.zeros((ROWS, 128), F32), jnp.zeros((ROWS, 128), F32))
    for k in range(LEVELS):
        wet = sea[k].astype(F32)
        edges = place_level(edges, k, thermal[k] * wet, zonal[k], meridian[k], wet)
    edges = place(edges, depth[...].astype(F32), DEPTH_LANE, WIDE)
    high[...], low[...] = edges


def pack_corners_kernel(south_edge, north_edge, to_east, to_west):
    for edge, start in ((south_edge, 0), (north_edge, 8)):
        edges = (jnp.zeros((8, 128), F32), jnp.zeros((8, 128), F32))
        for k in range(LEVELS):
            edges = place_level(
                edges, k, edge[k], edge[LEVELS + k], turn(edge[k], 4, 0), turn(edge[LEVELS + k], 4, 0)
            )
        edges = place(edges, edge[2 * LEVELS], DEPTH_LANE, WIDE)
        to_east[start : start + 8], to_west[start : start + 8] = edges


def with_corners(edge, corner):
    return jnp.concatenate([corner[:8], edge[...], corner[8:]], axis=0)


def rows_extended(inside, south_tile, north_tile, second):
    if second:
        south_tile = turn(south_tile, 4, 0)
        north_tile = turn(north_tile, 4, 0)
    return jnp.concatenate([south_tile, inside, north_tile], axis=0)


def edge_columns(west_tile, east_tile, lane_start, wide):
    ahead = turn(east_tile, -lane_start, 1)
    behind = turn(west_tile, 128 - wide - lane_start, 1)
    return jnp.where(iota(ahead.shape, 1) < 64, ahead, behind)


def face_value(here, ahead, behind, second):
    return (TRANSPORT_TICK / 12.0) * (7.0 * (here + ahead) - (behind + second))


def closure_kernel(
    thermal, sea, depth, adjoint, south_edge, north_edge, west_edge, east_edge,
    w1, b1, w2, b2, w3, b3,
    base, east_face, north_face, sums,
    tracer_ext, tracer_cols, w1_big, w2_pair, w2_pair_t, w3_big, w3_t, b1_wide, b2_wide,
    first0, left0, second0, slope10, slope20, outer0,
    first1, left1, second1, slope11, slope21, outer1,
    grad, grad_outer, bias1, bias2, bias3,
):
    for k in range(LEVELS):
        tracer_ext[k, 0:8] = south_edge[k]
        tracer_ext[k, 8 : ROWS + 8] = thermal[k] * sea[k].astype(F32)
        tracer_ext[k, ROWS + 8 :] = north_edge[k]
        tracer_cols[k] = edge_columns(
            west_edge[...], east_edge[...], TRACER_LANE + TRACER_WIDE * k, TRACER_WIDE
        )
    hidden_weight = w2[...].astype(BF16)
    outer_weight = w3[...].astype(BF16)
    spread = (iota((FIN, 8 * FIN), 1) // 8 == iota((FIN, 8 * FIN), 0)).astype(BF16)
    inner_wide = lax.dot_general(
        w1[...].astype(BF16), spread, (((0,), (0,)), ((), ())), preferred_element_type=F32
    )
    lane1 = iota((HID, 8 * FIN), 1)
    feature_lane = iota((FIN, 8 * FIN), 1) - 8 * iota((FIN, 8 * FIN), 0)
    spread3 = (iota((LEVELS, 64), 1) // 8 == iota((LEVELS, 64), 0)).astype(BF16)
    outer_tall = lax.dot_general(
        spread3, outer_weight, (((0,), (0,)), ((), ())), preferred_element_type=F32
    )
    outer_wide = lax.dot_general(
        outer_weight, spread3, (((0,), (0,)), ((), ())), preferred_element_type=F32
    )
    lane3 = iota((HID, 64), 1)
    row3 = iota((64, HID), 0)
    for r in range(8):
        w1_big[r * (HID + FIN) : r * (HID + FIN) + HID] = jnp.where(
            lane1 % 8 == r, inner_wide, 0.0
        ).astype(BF16)
        w1_big[r * (HID + FIN) + HID : (r + 1) * (HID + FIN)] = (feature_lane == r).astype(BF16)
        w3_t[r * HID : (r + 1) * HID] = jnp.where(lane3 % 8 == r, outer_wide, 0.0).astype(BF16)
        w3_big[:, r * HID : (r + 1) * HID] = jnp.where(row3 % 8 == r, outer_tall, 0.0).astype(BF16)
    blank = jnp.zeros((HID, HID), BF16)
    flipped = w2[...].T.astype(BF16)
    w2_pair[...] = jnp.concatenate(
        [jnp.concatenate([hidden_weight, blank], 1), jnp.concatenate([blank, hidden_weight], 1)], 0
    )
    w2_pair_t[...] = jnp.concatenate(
        [jnp.concatenate([flipped, blank], 1), jnp.concatenate([blank, flipped], 1)], 0
    )
    for bias, wide_bias in ((b1, b1_wide), (b2, b2_wide)):
        tall_bias = jnp.broadcast_to(bias[...], (HID, HID)).T
        wide_bias[...] = jnp.concatenate([tall_bias, tall_bias], 1)
    grad[...] = jnp.zeros_like(grad)
    grad_outer[...] = jnp.zeros_like(grad_outer)
    bias1[...] = jnp.zeros_like(bias1)
    bias2[...] = jnp.zeros_like(bias2)
    bias3[...] = jnp.zeros_like(bias3)
    level = iota((LEVELS, 8, COLS), 0).astype(F32)
    tall = tracer_ext[:, 0:24, :]
    ahead = north(tall)
    north_face[:, 0:8, :] = face_value(
        tall[:, 0:8], ahead[:, 0:8], south(tall)[:, 0:8], north(ahead)[:, 0:8]
    )
    b3_cube = jnp.concatenate([jnp.full((1, 8, COLS), b3[k], F32) for k in range(LEVELS)], 0)

    def forward(j, first, left, second, slope1, slope2, outer):
        start = pl.multiple_of(j * 8, 8)
        tall = tracer_ext[:, pl.ds(start, 24), :]
        tracer = tall[:, 8:16]
        wet = sea[:, pl.ds(start, 8), :].astype(F32)
        floor = depth[pl.ds(start, 8), :].astype(F32)
        wide = jnp.concatenate([tracer, tracer_cols[:, pl.ds(start, 8), :]], axis=2)
        ahead, behind = east(wide), west(wide)
        zonal_slope = 0.5 * (ahead[:, :, :COLS] - behind[:, :, :COLS])
        east_face[:, pl.ds(start, 8), :] = face_value(wide, ahead, behind, east(ahead))
        ahead, behind = north(tall), south(tall)
        meridian_slope = 0.5 * (ahead[:, 8:16] - behind[:, 8:16])
        north_face[:, pl.ds(start + 8, 8), :] = face_value(
            tracer, ahead[:, 8:16], behind[:, 8:16], north(ahead)[:, 8:16]
        )
        clearance = wet * (floor[None] - level) * (1.0 / LEVELS)
        features = (
            jnp.concatenate([tracer, zonal_slope, meridian_slope, clearance], axis=0)
            .reshape(8 * FIN, COLS)
            .astype(BF16)
        )
        yield
        for p in range(4):
            z = dot(w1_big[p * 2 * (HID + FIN) : (p + 1) * 2 * (HID + FIN)], features)
            for q in range(2):
                r = 2 * p + q
                z0 = q * (HID + FIN)
                value = jnp.tanh(z[z0 : z0 + HID] + b1_wide[...])
                first[r * HID : (r + 1) * HID] = value.astype(BF16)
                slope1[r] = 1.0 - value * value
                left[r, HID:] = z[z0 + HID : z0 + HID + FIN].astype(BF16)
            yield
        for p in range(4):
            z = dot(w2_pair[...], first[p * 2 * HID : (p + 1) * 2 * HID])
            for q in range(2):
                r = 2 * p + q
                value = jnp.tanh(z[q * HID : (q + 1) * HID] + b2_wide[...])
                second[r * HID : (r + 1) * HID] = value.astype(BF16)
                slope2[r] = 1.0 - value * value
            yield
        squash = jax.nn.sigmoid(
            dot(w3_big[...], second[...]).reshape(LEVELS, 8, COLS) + b3_cube
        )
        kappa = KAPPA_FLOOR + KAPPA_SPAN * squash
        jump = tracer[1:] - tracer[:-1]
        pair_jump = wet[:-1] * wet[1:] * jump
        adj = adjoint[:, pl.ds(start, 8), :]
        bond = pair_jump * (adj[:-1] - adj[1:])
        none = jnp.zeros((1, 8, COLS), F32)
        pull = 0.5 * (jnp.concatenate([bond, none], 0) + jnp.concatenate([none, bond], 0))
        down = 0.5 * (kappa[:-1] + kappa[1:]) * pair_jump
        mixing = jnp.concatenate([down, none], 0) - jnp.concatenate([none, down], 0)
        base[:, pl.ds(start, 8), :] = tracer + mixing
        outer[...] = pull * KAPPA_SPAN * squash * (1.0 - squash)

    def backward(first, left, second, slope1, slope2, outer):
        outer_term = outer[...]
        bias3[...] += outer_term
        outer_grad = outer_term.reshape(64, COLS).astype(BF16)
        total1 = bias1[...]
        total2 = bias2[...]
        terms = []
        for p in range(4):
            back = dot(w3_t[p * 2 * HID : (p + 1) * 2 * HID], outer_grad)
            for q in range(2):
                r = 2 * p + q
                hidden_term = back[q * HID : (q + 1) * HID] * slope2[r]
                total2 = total2 + hidden_term
                left[r, :HID] = hidden_term.astype(BF16)
            cols = slice(p * 2 * HID, (p + 1) * 2 * HID)
            grad_outer[:, cols] += dot_nt(outer_grad, second[cols])
            yield
        bias2[...] = total2
        total = grad[...]
        rights = []
        for p in range(4):
            z = dot(w2_pair_t[...], jnp.concatenate([left[2 * p, :HID], left[2 * p + 1, :HID]], 0))
            for q in range(2):
                r = 2 * p + q
                inner_term = z[q * HID : (q + 1) * HID] * slope1[r]
                total1 = total1 + inner_term
                rights.append(jnp.concatenate(
                    [inner_term.astype(BF16), first[r * HID : (r + 1) * HID]], 0
                ))
            if p:
                for r in (2 * p - 2, 2 * p - 1):
                    total = total + dot_nt(left[r], rights[r])
            yield
        yield
        for r in (6, 7):
            total = total + dot_nt(left[r], rights[r])
        bias1[...] = total1
        grad[...] = total

    def together(*parts):
        parts = list(parts)
        while parts:
            for part in list(parts):
                if next(part, parts) is parts:
                    parts.remove(part)

    even = (first0, left0, second0, slope10, slope20, outer0)
    odd = (first1, left1, second1, slope11, slope21, outer1)
    together(forward(0, *even))

    def step(i, carry):
        together(forward(2 * i + 1, *odd), backward(*even))
        together(forward(jnp.minimum(2 * i + 2, BLOCKS - 1), *even), backward(*odd))
        return carry

    lax.fori_loop(0, BLOCKS // 2 - 1, step, 0)
    together(forward(BLOCKS - 1, *odd), backward(*even))
    together(backward(*odd))
    sums[0:HID] = grad[0:HID, HID:]
    sums[ROW_INNER : ROW_INNER + FIN] = grad[HID:, :HID]
    row_outer = iota((64, HID), 0)
    outer_sum = jnp.zeros((64, HID), F32)
    for r in range(8):
        outer_sum = outer_sum + jnp.where(
            row_outer % 8 == r, grad_outer[:, r * HID : (r + 1) * HID], 0.0
        )
    sums[ROW_OUTER : ROW_OUTER + LEVELS] = jnp.sum(outer_sum.reshape(LEVELS, 8, HID), axis=1)
    outer_bias = jnp.sum(bias3[...], axis=1)
    sums[ROW_OUTER_BIAS : ROW_OUTER_BIAS + LEVELS] = outer_bias[:, :128] + outer_bias[:, 128:]
    inner_row_sum = jnp.sum((bias1[:, :128] + bias1[:, 128:]).T, axis=0, keepdims=True)
    hidden_row_sum = jnp.sum((bias2[:, :128] + bias2[:, 128:]).T, axis=0, keepdims=True)
    sums[ROW_BIAS:] = jnp.concatenate(
        [inner_row_sum, hidden_row_sum, jnp.zeros((SUM_ROWS - ROW_BIAS - 2, 128), F32)], 0
    )


def field_extended(inside, south_tile, north_tile, second, west_tile, east_tile, lane_start, wide):
    tall = rows_extended(inside, south_tile, north_tile, second)
    return jnp.concatenate([tall, edge_columns(west_tile, east_tile, lane_start, wide)], axis=1)


def gram_kernel(
    zonal, meridian, sea, depth, south_edge, north_edge, west_edge, east_edge, west_corner, east_corner,
    sums,
    basis, parts, east_open, north_open,
    east_transport, north_transport, east_bits, north_bits,
):
    west_tile = with_corners(west_edge, west_corner)
    east_tile = with_corners(east_edge, east_corner)

    def extended(inside, index, second, lane_start):
        return field_extended(
            inside, south_edge[index], north_edge[index], second,
            west_tile, east_tile, lane_start, WIDE,
        )

    def gather(k, carry):
        wet = extended(sea[k].astype(F32), LEVELS + k, True, WET_LANE + WIDE * k)
        east_pair = wet * east(wet)
        north_pair = wet * north(wet)
        east_transport[...] += east_pair * extended(
            zonal[k], LEVELS + k, False, ZONAL_LANE + WIDE * k
        )
        north_transport[...] += north_pair * extended(
            meridian[k], k, True, MERIDIAN_LANE + WIDE * k
        )
        place_value = lax.shift_left(jnp.int32(1), k).astype(F32)
        east_bits[...] += east_pair[8 : ROWS + 8] * place_value
        north_bits[...] += north_pair[:, :COLS] * place_value
        return carry

    for total in (east_transport, north_transport, east_bits, north_bits):
        total[...] = jnp.zeros_like(total)
    lax.fori_loop(0, LEVELS, gather, 0)
    east_open[...] = east_bits[...].astype(jnp.int32)
    north_open[...] = north_bits[...].astype(jnp.int32)
    source = -(
        (east_transport[...] - west(east_transport[...]))
        + (north_transport[...] - south(north_transport[...]))
    )
    floor = extended(depth[...].astype(F32), 2 * LEVELS, False, DEPTH_LANE)
    east_depth = jnp.minimum(floor, east(floor))
    north_depth = jnp.minimum(floor, north(floor))
    west_depth = west(east_depth)
    south_depth = south(north_depth)

    def operate(field):
        return (
            SIGMA * field
            + east_depth * (field - east(field))
            + west_depth * (field - west(field))
            + north_depth * (field - north(field))
            + south_depth * (field - south(field))
        )

    image0 = operate(source)
    first = (image0 - CENTRE * source) * (1.0 / HALF_WIDTH)
    image1 = operate(first)
    second = (image1 - CENTRE * first) * (2.0 / HALF_WIDTH) - source
    image2 = operate(second)
    basis[0] = source
    basis[1] = first
    basis[2] = second

    lane = iota((1, 128), 1)
    gram = jnp.zeros((1, 128), F32)
    pairs = (
        (source, image0), (first, image0), (second, image0),
        (first, image1), (second, image1), (second, image2),
        (source, source), (first, source), (second, source),
    )
    for i, (a, b) in enumerate(pairs):
        total = jnp.sum(a[8 : ROWS + 8, :COLS] * b[8 : ROWS + 8, :COLS], axis=0, keepdims=True)
        gram = jnp.where(lane == i, jnp.sum(total, axis=1, keepdims=True), gram)
    count, tall, _ = parts.shape
    own = SUM_ROWS // count
    tail = jnp.broadcast_to(gram, (tall - own, 128))
    for i in range(count):
        parts[i, :own] = sums[i * own : (i + 1) * own]
        parts[i, own:] = tail


def galerkin(h00, h01, h02, h11, h12, h22, g0, g1, g2):
    tiny = 1e-6

    def pivot(value, scale):
        good = value > tiny * scale
        return jnp.where(good, 1.0 / jnp.where(good, value, 1.0), 0.0)

    p0 = pivot(h00, 0.0)
    l10 = h01 * p0
    l20 = h02 * p0
    d1 = h11 - l10 * h01
    p1 = pivot(d1, h11)
    s21 = h12 - l20 * h01
    l21 = s21 * p1
    d2 = h22 - l20 * h02 - l21 * s21
    p2 = pivot(d2, h22)
    z0 = g0
    z1 = g1 - l10 * z0
    z2 = g2 - l20 * z0 - l21 * z1
    y2 = z2 * p2
    y1 = z1 * p1 - l21 * y2
    y0 = z0 * p0 - l10 * y1 - l20 * y2
    return y0, y1, y2


def final_kernel(
    scale, zonal, meridian, base, east_face, north_face, south_edge, west_edge, basis, east_open, north_open,
    parts,
    revised_far, height_out, grad1, bias1, grad2, bias2, grad3, bias3,
    revised, falls, totals, sent,
):
    def store(k):
        return pltpu.make_async_copy(revised.at[k], revised_far.at[k], sent.at[k])

    count = parts.shape[0]
    own = SUM_ROWS // count
    gram = parts[0, own : own + 1]
    y0, y1, y2 = galerkin(*[gram[:, i : i + 1] for i in range(9)])
    height = y0 * basis[0] + y1 * basis[1] + y2 * basis[2]
    height_out[...] = height[8 : ROWS + 8, :COLS]
    falls[0] = east(height) - height
    falls[1] = north(height) - height
    tall = ROWS + 8

    def level(k, carry):
        bit = lax.shift_left(jnp.int32(1), k)
        u = jnp.concatenate([zonal[k], turn(west_edge[...], 128 - WIDE - ZONAL_LANE - WIDE * k, 1)], 1)
        v = jnp.concatenate([turn(south_edge[k], 4, 0), meridian[k]], 0)
        flux = jnp.where((east_open[...] & bit) != 0, (u - falls[0, 8 : ROWS + 8]) * east_face[k], 0.0)
        spread = (flux - west(flux))[:, :COLS]
        flux = jnp.where((north_open[:tall] & bit) != 0, (v - falls[1, :tall, :COLS]) * north_face[k], 0.0)
        spread = spread + (flux - south(flux))[8:]
        revised[k] = base[k] - spread
        store(k).start()
        return carry

    lax.fori_loop(0, LEVELS, level, 0)
    for i in range(count):
        totals[i * own : (i + 1) * own] = parts[i, :own] * scale
    grad2[...] = totals[0:HID]
    grad1[...] = totals[ROW_INNER : ROW_INNER + FIN]
    grad3[...] = totals[ROW_OUTER : ROW_OUTER + LEVELS]
    bias1[...] = totals[ROW_BIAS : ROW_BIAS + 1]
    bias2[...] = totals[ROW_BIAS + 1 : ROW_BIAS + 2]
    outer_bias = jnp.sum(totals[ROW_OUTER_BIAS : ROW_OUTER_BIAS + LEVELS], axis=1, keepdims=True)
    diagonal = iota((LEVELS, LEVELS), 0) == iota((LEVELS, LEVELS), 1)
    bias3[...] = jnp.sum(jnp.where(diagonal, outer_bias, 0.0), axis=0, keepdims=True)
    for k in range(LEVELS):
        store(k).wait()


def struct(*shape, dtype=F32):
    return jax.ShapeDtypeStruct(shape, dtype)


def call(kernel, out_shape, scratch=(), mib=16, flops=0, transcendentals=0, nbytes=0, **specs):
    return pl.pallas_call(
        kernel,
        out_shape=out_shape,
        scratch_shapes=list(scratch),
        compiler_params=pltpu.CompilerParams(vmem_limit_bytes=mib * 1024 * 1024),
        cost_estimate=pl.CostEstimate(
            flops=flops, transcendentals=transcendentals, bytes_accessed=nbytes
        ),
        **specs,
    )


def near(count):
    return [pl.BlockSpec(memory_space=pltpu.VMEM)] * count


def far(count):
    return [pl.BlockSpec(memory_space=pltpu.HBM)] * count


def sum_kernel(parts, copies):
    total = parts[0]
    for i in range(1, parts.shape[0]):
        total = total + parts[i]
    for i in range(copies.shape[0]):
        copies[i] = total


def summed_copies(parts, count):
    return call(sum_kernel, struct(count, *parts.shape[1:]), mib=4, nbytes=300_000)(parts)


def local(thermal, zonal, meridian, sea, depth, adjoint, w1, b1, w2, b2, w3, b3):
    lons, lats = lax.axis_size("lon"), lax.axis_size("lat")
    ring = [(i, (i + 1) % lons) for i in range(lons)]
    line = [(i, i + 1) for i in range(lats - 1)]

    def back(pairs):
        return [(target, source) for source, target in pairs]

    to_north, to_south = call(
        pack_rows_kernel,
        (struct(17, 8, COLS), struct(17, 8, COLS)),
        scratch=[
            pltpu.VMEM((6, LEVELS, 8, COLS), F32),
            pltpu.VMEM((2, LEVELS, 8, COLS), jnp.int32),
            pltpu.VMEM((2, 8, COLS), jnp.int32),
            pltpu.SemaphoreType.DMA((10,)),
        ],
        in_specs=far(5),
        mib=58,
        nbytes=1_000_000,
    )(thermal, zonal, meridian, sea, depth)
    south_edge = lax.ppermute(to_north, "lat", line)
    north_edge = lax.ppermute(to_south, "lat", back(line))
    high, low = call(
        pack_columns_kernel,
        (struct(ROWS, 128), struct(ROWS, 128)),
        mib=8,
        flops=4_000_000,
        nbytes=5_000_000,
    )(thermal, zonal, meridian, sea, depth)
    west_edge = lax.ppermute(high, "lon", ring)
    east_edge = lax.ppermute(low, "lon", back(ring))
    to_east, to_west = call(
        pack_corners_kernel,
        (struct(16, 128), struct(16, 128)),
        mib=4,
        nbytes=400_000,
    )(south_edge, north_edge)
    west_corner = lax.ppermute(to_east, "lon", ring)
    east_corner = lax.ppermute(to_west, "lon", back(ring))

    base, east_face, north_face, sums = call(
        closure_kernel,
        (
            struct(LEVELS, ROWS, COLS),
            struct(LEVELS, ROWS, EXT_COLS),
            struct(LEVELS, ROWS + 8, COLS),
            struct(SUM_ROWS, 128),
        ),
        scratch=[
            pltpu.VMEM((LEVELS, EXT_ROWS, COLS), F32),
            pltpu.VMEM((LEVELS, ROWS, 128), F32),
            pltpu.VMEM((8 * (HID + FIN), 8 * FIN), BF16),
            pltpu.VMEM((2 * HID, 2 * HID), BF16),
            pltpu.VMEM((2 * HID, 2 * HID), BF16),
            pltpu.VMEM((64, 8 * HID), BF16),
            pltpu.VMEM((8 * HID, 64), BF16),
            pltpu.VMEM((HID, COLS), F32),
            pltpu.VMEM((HID, COLS), F32),
        ]
        + 2
        * [
            pltpu.VMEM((8 * HID, COLS), BF16),
            pltpu.VMEM((8, HID + FIN, COLS), BF16),
            pltpu.VMEM((8 * HID, COLS), BF16),
            pltpu.VMEM((8, HID, COLS), F32),
            pltpu.VMEM((8, HID, COLS), F32),
            pltpu.VMEM((LEVELS, 8, COLS), F32),
        ]
        + [
            pltpu.VMEM((HID + FIN, COLS), F32),
            pltpu.VMEM((64, 8 * HID), F32),
            pltpu.VMEM((HID, COLS), F32),
            pltpu.VMEM((HID, COLS), F32),
            pltpu.VMEM((LEVELS, 8, COLS), F32),
        ],
        in_specs=near(13) + [pl.BlockSpec(memory_space=pltpu.SMEM)],
        mib=24,
        flops=8_000_000_000,
        transcendentals=9_000_000,
        nbytes=5_000_000,
    )(
        thermal, sea, depth, adjoint, south_edge, north_edge, west_edge, east_edge,
        w1.T, b1[None], w2, b2[None], w3, b3,
    )
    basis, parts, east_open, north_open = call(
        gram_kernel,
        (
            struct(3, EXT_ROWS, EXT_COLS),
            struct(lons, (SUM_ROWS // lons // 8 + 1) * 8, 128),
            struct(ROWS, EXT_COLS, dtype=jnp.int32),
            struct(EXT_ROWS, COLS, dtype=jnp.int32),
        ),
        scratch=[pltpu.VMEM((EXT_ROWS, EXT_COLS), F32)] * 2
        + [pltpu.VMEM((ROWS, EXT_COLS), F32), pltpu.VMEM((EXT_ROWS, COLS), F32)],
        flops=20_000_000,
        nbytes=5_000_000,
    )(
        zonal, meridian, sea, depth, south_edge, north_edge, west_edge, east_edge, west_corner, east_corner,
        sums,
    )
    parts = lax.all_to_all(parts, "lon", 0, 0)
    parts = lax.all_to_all(summed_copies(parts, lats), "lat", 0, 0)
    parts = lax.all_to_all(summed_copies(parts, lons), "lon", 0, 0)
    scale = GRADIENT_GAIN / math.sqrt(ROWS * lats * COLS * lons)
    revised, height, grad1, bias1, grad2, bias2, grad3, bias3 = call(
        functools.partial(final_kernel, scale),
        (
            struct(LEVELS, ROWS, COLS),
            struct(ROWS, COLS),
            struct(FIN, HID),
            struct(1, HID),
            struct(HID, HID),
            struct(1, HID),
            struct(LEVELS, HID),
            struct(1, LEVELS),
        ),
        scratch=[
            pltpu.VMEM((LEVELS, ROWS, COLS), F32),
            pltpu.VMEM((2, EXT_ROWS, EXT_COLS), F32),
            pltpu.VMEM((SUM_ROWS, 128), F32),
            pltpu.SemaphoreType.DMA((LEVELS,)),
        ],
        out_specs=tuple(far(1) + near(7)),
        flops=20_000_000,
        nbytes=8_000_000,
    )(
        zonal, meridian, base, east_face, north_face, south_edge, west_edge, basis, east_open, north_open, parts,
    )
    return (
        revised,
        height,
        grad1.T,
        bias1.reshape(HID),
        grad2,
        bias2.reshape(HID),
        grad3,
        bias3.reshape(LEVELS),
    )


def solution(mesh):
    cube, plane, whole = P(None, "lat", "lon"), P("lat", "lon"), P()
    return jax.shard_map(
        local,
        mesh=mesh,
        in_specs=(cube, cube, cube, cube, plane, cube) + (whole,) * 6,
        out_specs=(cube, plane) + (whole,) * 6,
        check_vma=False,
    )
```

```python
import functools
import math

import jax
import jax.numpy as jnp
from jax import lax
from jax.experimental import pallas as pl
from jax.experimental.pallas import tpu as pltpu
from jax.sharding import PartitionSpec as P

LEVELS = 8
HID = 128
FIN = 32
ROWS = 128
COLS = 256
EXT_ROWS = ROWS + 16
EXT_COLS = COLS + 128
BLOCKS = ROWS // 8

SIGMA = 0.5
TRANSPORT_TICK = 0.2
KAPPA_FLOOR = 0.02
KAPPA_SPAN = 0.4
GRADIENT_GAIN = 16.0

CENTRE = 32.5
HALF_WIDTH = 32.0

TRACER_LANE, TRACER_WIDE = 0, 2
ZONAL_LANE, MERIDIAN_LANE, WET_LANE, DEPTH_LANE, WIDE = 16, 48, 80, 112, 4

ROW_INNER = 128
ROW_OUTER = 160
ROW_OUTER_BIAS = 168
ROW_BIAS = 176
SUM_ROWS = 192

F32 = jnp.float32
BF16 = jnp.bfloat16


def iota(shape, axis):
    return lax.broadcasted_iota(jnp.int32, shape, axis)


def turn(value, shift, axis):
    if isinstance(shift, int):
        shift %= value.shape[axis]
        return pltpu.roll(value, shift, axis) if shift else value
    return pltpu.roll(value, lax.rem(shift + value.shape[axis], value.shape[axis]), axis)


def east(value):
    return turn(value, -1, value.ndim - 1)


def west(value):
    return turn(value, 1, value.ndim - 1)


def north(value):
    return turn(value, -1, value.ndim - 2)


def south(value):
    return turn(value, 1, value.ndim - 2)


def dot(left, right):
    return lax.dot_general(left, right, (((1,), (0,)), ((), ())), preferred_element_type=F32)


def dot_nt(left, right):
    return lax.dot_general(left, right, (((1,), (1,)), ((), ())), preferred_element_type=F32)


def pack_rows_kernel(
    thermal_far, zonal_far, meridian_far, sea_far, depth_far,
    to_north, to_south,
    floats, seas, floors, arrived,
):
    copies = []
    for side, start in enumerate((ROWS - 8, 0)):
        rows = pl.ds(start, 8)
        pairs = [
            (thermal_far.at[:, rows], floats.at[3 * side]),
            (zonal_far.at[:, rows], floats.at[3 * side + 1]),
            (meridian_far.at[:, rows], floats.at[3 * side + 2]),
            (sea_far.at[:, rows], seas.at[side]),
            (depth_far.at[rows], floors.at[side]),
        ]
        copies += [
            pltpu.make_async_copy(source, target, arrived.at[5 * side + i])
            for i, (source, target) in enumerate(pairs)
        ]
    for copy in copies:
        copy.start()
    for copy in copies:
        copy.wait()
    low = iota((8, COLS), 0) < 4
    for k in range(LEVELS):
        wet = seas[0, k].astype(F32)
        to_north[k] = jnp.where(low, turn(floats[2, k], 4, 0), floats[0, k] * wet)
        to_north[LEVELS + k] = jnp.where(low, turn(wet, 4, 0), floats[1, k])
        wet = seas[1, k].astype(F32)
        to_south[k] = jnp.where(low, floats[3, k] * wet, turn(floats[5, k], 4, 0))
        to_south[LEVELS + k] = jnp.where(low, floats[4, k], turn(wet, 4, 0))
    to_north[2 * LEVELS] = floors[0].astype(F32)
    to_south[2 * LEVELS] = floors[1].astype(F32)


def place(edges, field, lane_start, wide):
    lane = iota((field.shape[0], 128), 1)
    mask = jnp.logical_and(lane >= lane_start, lane < lane_start + wide)
    high = jnp.where(mask, turn(field[:, 128:], lane_start + wide, 1), edges[0])
    low = jnp.where(mask, turn(field[:, :128], lane_start, 1), edges[1])
    return high, low


def place_level(edges, k, tracer, u, v, wet):
    edges = place(edges, tracer, TRACER_LANE + TRACER_WIDE * k, TRACER_WIDE)
    edges = place(edges, u, ZONAL_LANE + WIDE * k, WIDE)
    edges = place(edges, v, MERIDIAN_LANE + WIDE * k, WIDE)
    return place(edges, wet, WET_LANE + WIDE * k, WIDE)


def pack_columns_kernel(thermal, zonal, meridian, sea, depth, high, low):
    edges = (jnp.zeros((ROWS, 128), F32), jnp.zeros((ROWS, 128), F32))
    for k in range(LEVELS):
        wet = sea[k].astype(F32)
        edges = place_level(edges, k, thermal[k] * wet, zonal[k], meridian[k], wet)
    edges = place(edges, depth[...].astype(F32), DEPTH_LANE, WIDE)
    high[...], low[...] = edges


def pack_corners_kernel(south_edge, north_edge, to_east, to_west):
    for edge, start in ((south_edge, 0), (north_edge, 8)):
        edges = (jnp.zeros((8, 128), F32), jnp.zeros((8, 128), F32))
        for k in range(LEVELS):
            edges = place_level(
                edges, k, edge[k], edge[LEVELS + k], turn(edge[k], 4, 0), turn(edge[LEVELS + k], 4, 0)
            )
        edges = place(edges, edge[2 * LEVELS], DEPTH_LANE, WIDE)
        to_east[start : start + 8], to_west[start : start + 8] = edges


def with_corners(edge, corner):
    return jnp.concatenate([corner[:8], edge[...], corner[8:]], axis=0)


def rows_extended(inside, south_tile, north_tile, second):
    if second:
        south_tile = turn(south_tile, 4, 0)
        north_tile = turn(north_tile, 4, 0)
    return jnp.concatenate([south_tile, inside, north_tile], axis=0)


def edge_columns(west_tile, east_tile, lane_start, wide):
    ahead = turn(east_tile, -lane_start, 1)
    behind = turn(west_tile, 128 - wide - lane_start, 1)
    return jnp.where(iota(ahead.shape, 1) < 64, ahead, behind)


def face_value(here, ahead, behind, second):
    return (TRANSPORT_TICK / 12.0) * (7.0 * (here + ahead) - (behind + second))


def closure_kernel(
    thermal, sea, depth, adjoint, south_edge, north_edge, west_edge, east_edge,
    w1, b1, w2, b2, w3, b3,
    base, east_face, north_face, sums,
    tracer_ext, tracer_cols, w1_big, w2_pair, w2_pair_t, w3_big, w3_t, b1_wide, b2_wide,
    first0, left0, second0, slope10, slope20, outer0,
    first1, left1, second1, slope11, slope21, outer1,
    grad, grad_outer, bias1, bias2, bias3,
):
    for k in range(LEVELS):
        tracer_ext[k, 0:8] = south_edge[k]
        tracer_ext[k, 8 : ROWS + 8] = thermal[k] * sea[k].astype(F32)
        tracer_ext[k, ROWS + 8 :] = north_edge[k]
        tracer_cols[k] = edge_columns(
            west_edge[...], east_edge[...], TRACER_LANE + TRACER_WIDE * k, TRACER_WIDE
        )
    hidden_weight = w2[...].astype(BF16)
    outer_weight = w3[...].astype(BF16)
    spread = (iota((FIN, 8 * FIN), 1) // 8 == iota((FIN, 8 * FIN), 0)).astype(BF16)
    inner_wide = lax.dot_general(
        w1[...].astype(BF16), spread, (((0,), (0,)), ((), ())), preferred_element_type=F32
    )
    lane1 = iota((HID, 8 * FIN), 1)
    feature_lane = iota((FIN, 8 * FIN), 1) - 8 * iota((FIN, 8 * FIN), 0)
    spread3 = (iota((LEVELS, 64), 1) // 8 == iota((LEVELS, 64), 0)).astype(BF16)
    outer_tall = lax.dot_general(
        spread3, outer_weight, (((0,), (0,)), ((), ())), preferred_element_type=F32
    )
    outer_wide = lax.dot_general(
        outer_weight, spread3, (((0,), (0,)), ((), ())), preferred_element_type=F32
    )
    lane3 = iota((HID, 64), 1)
    row3 = iota((64, HID), 0)
    for r in range(8):
        w1_big[r * (HID + FIN) : r * (HID + FIN) + HID] = jnp.where(
            lane1 % 8 == r, inner_wide, 0.0
        ).astype(BF16)
        w1_big[r * (HID + FIN) + HID : (r + 1) * (HID + FIN)] = (feature_lane == r).astype(BF16)
        w3_t[r * HID : (r + 1) * HID] = jnp.where(lane3 % 8 == r, outer_wide, 0.0).astype(BF16)
        w3_big[:, r * HID : (r + 1) * HID] = jnp.where(row3 % 8 == r, outer_tall, 0.0).astype(BF16)
    blank = jnp.zeros((HID, HID), BF16)
    flipped = w2[...].T.astype(BF16)
    w2_pair[...] = jnp.concatenate(
        [jnp.concatenate([hidden_weight, blank], 1), jnp.concatenate([blank, hidden_weight], 1)], 0
    )
    w2_pair_t[...] = jnp.concatenate(
        [jnp.concatenate([flipped, blank], 1), jnp.concatenate([blank, flipped], 1)], 0
    )
    for bias, wide_bias in ((b1, b1_wide), (b2, b2_wide)):
        tall_bias = jnp.broadcast_to(bias[...], (HID, HID)).T
        wide_bias[...] = jnp.concatenate([tall_bias, tall_bias], 1)
    grad[...] = jnp.zeros_like(grad)
    grad_outer[...] = jnp.zeros_like(grad_outer)
    bias1[...] = jnp.zeros_like(bias1)
    bias2[...] = jnp.zeros_like(bias2)
    bias3[...] = jnp.zeros_like(bias3)
    level = iota((LEVELS, 8, COLS), 0).astype(F32)
    tall = tracer_ext[:, 0:24, :]
    ahead = north(tall)
    north_face[:, 0:8, :] = face_value(
        tall[:, 0:8], ahead[:, 0:8], south(tall)[:, 0:8], north(ahead)[:, 0:8]
    )
    b3_cube = jnp.concatenate([jnp.full((1, 8, COLS), b3[k], F32) for k in range(LEVELS)], 0)

    def forward(j, first, left, second, slope1, slope2, outer):
        start = pl.multiple_of(j * 8, 8)
        tall = tracer_ext[:, pl.ds(start, 24), :]
        tracer = tall[:, 8:16]
        wet = sea[:, pl.ds(start, 8), :].astype(F32)
        floor = depth[pl.ds(start, 8), :].astype(F32)
        wide = jnp.concatenate([tracer, tracer_cols[:, pl.ds(start, 8), :]], axis=2)
        ahead, behind = east(wide), west(wide)
        zonal_slope = 0.5 * (ahead[:, :, :COLS] - behind[:, :, :COLS])
        east_face[:, pl.ds(start, 8), :] = face_value(wide, ahead, behind, east(ahead))
        ahead, behind = north(tall), south(tall)
        meridian_slope = 0.5 * (ahead[:, 8:16] - behind[:, 8:16])
        north_face[:, pl.ds(start + 8, 8), :] = face_value(
            tracer, ahead[:, 8:16], behind[:, 8:16], north(ahead)[:, 8:16]
        )
        clearance = wet * (floor[None] - level) * (1.0 / LEVELS)
        features = (
            jnp.concatenate([tracer, zonal_slope, meridian_slope, clearance], axis=0)
            .reshape(8 * FIN, COLS)
            .astype(BF16)
        )
        yield
        for p in range(4):
            z = dot(w1_big[p * 2 * (HID + FIN) : (p + 1) * 2 * (HID + FIN)], features)
            for q in range(2):
                r = 2 * p + q
                z0 = q * (HID + FIN)
                value = jnp.tanh(z[z0 : z0 + HID] + b1_wide[...])
                first[r * HID : (r + 1) * HID] = value.astype(BF16)
                slope1[r] = 1.0 - value * value
                left[r, HID:] = z[z0 + HID : z0 + HID + FIN].astype(BF16)
            yield
        for p in range(4):
            z = dot(w2_pair[...], first[p * 2 * HID : (p + 1) * 2 * HID])
            for q in range(2):
                r = 2 * p + q
                value = jnp.tanh(z[q * HID : (q + 1) * HID] + b2_wide[...])
                second[r * HID : (r + 1) * HID] = value.astype(BF16)
                slope2[r] = 1.0 - value * value
            yield
        squash = jax.nn.sigmoid(
            dot(w3_big[...], second[...]).reshape(LEVELS, 8, COLS) + b3_cube
        )
        kappa = KAPPA_FLOOR + KAPPA_SPAN * squash
        jump = tracer[1:] - tracer[:-1]
        pair_jump = wet[:-1] * wet[1:] * jump
        adj = adjoint[:, pl.ds(start, 8), :]
        bond = pair_jump * (adj[:-1] - adj[1:])
        none = jnp.zeros((1, 8, COLS), F32)
        pull = 0.5 * (jnp.concatenate([bond, none], 0) + jnp.concatenate([none, bond], 0))
        down = 0.5 * (kappa[:-1] + kappa[1:]) * pair_jump
        mixing = jnp.concatenate([down, none], 0) - jnp.concatenate([none, down], 0)
        base[:, pl.ds(start, 8), :] = tracer + mixing
        outer[...] = pull * KAPPA_SPAN * squash * (1.0 - squash)

    def backward(first, left, second, slope1, slope2, outer):
        outer_term = outer[...]
        bias3[...] += outer_term
        outer_grad = outer_term.reshape(64, COLS).astype(BF16)
        total1 = bias1[...]
        total2 = bias2[...]
        terms = []
        for p in range(4):
            back = dot(w3_t[p * 2 * HID : (p + 1) * 2 * HID], outer_grad)
            for q in range(2):
                r = 2 * p + q
                hidden_term = back[q * HID : (q + 1) * HID] * slope2[r]
                total2 = total2 + hidden_term
                left[r, :HID] = hidden_term.astype(BF16)
            cols = slice(p * 2 * HID, (p + 1) * 2 * HID)
            grad_outer[:, cols] += dot_nt(outer_grad, second[cols])
            yield
        bias2[...] = total2
        total = grad[...]
        rights = []
        for p in range(4):
            z = dot(w2_pair_t[...], jnp.concatenate([left[2 * p, :HID], left[2 * p + 1, :HID]], 0))
            for q in range(2):
                r = 2 * p + q
                inner_term = z[q * HID : (q + 1) * HID] * slope1[r]
                total1 = total1 + inner_term
                rights.append(jnp.concatenate(
                    [inner_term.astype(BF16), first[r * HID : (r + 1) * HID]], 0
                ))
            if p:
                for r in (2 * p - 2, 2 * p - 1):
                    total = total + dot_nt(left[r], rights[r])
            yield
        yield
        for r in (6, 7):
            total = total + dot_nt(left[r], rights[r])
        bias1[...] = total1
        grad[...] = total

    def together(*parts):
        parts = list(parts)
        while parts:
            for part in list(parts):
                if next(part, parts) is parts:
                    parts.remove(part)

    even = (first0, left0, second0, slope10, slope20, outer0)
    odd = (first1, left1, second1, slope11, slope21, outer1)
    together(forward(0, *even))

    def step(i, carry):
        together(forward(2 * i + 1, *odd), backward(*even))
        together(forward(jnp.minimum(2 * i + 2, BLOCKS - 1), *even), backward(*odd))
        return carry

    lax.fori_loop(0, BLOCKS // 2 - 1, step, 0)
    together(forward(BLOCKS - 1, *odd), backward(*even))
    together(backward(*odd))
    sums[0:HID] = grad[0:HID, HID:]
    sums[ROW_INNER : ROW_INNER + FIN] = grad[HID:, :HID]
    row_outer = iota((64, HID), 0)
    outer_sum = jnp.zeros((64, HID), F32)
    for r in range(8):
        outer_sum = outer_sum + jnp.where(
            row_outer % 8 == r, grad_outer[:, r * HID : (r + 1) * HID], 0.0
        )
    sums[ROW_OUTER : ROW_OUTER + LEVELS] = jnp.sum(outer_sum.reshape(LEVELS, 8, HID), axis=1)
    outer_bias = jnp.sum(bias3[...], axis=1)
    sums[ROW_OUTER_BIAS : ROW_OUTER_BIAS + LEVELS] = outer_bias[:, :128] + outer_bias[:, 128:]
    inner_row_sum = jnp.sum((bias1[:, :128] + bias1[:, 128:]).T, axis=0, keepdims=True)
    hidden_row_sum = jnp.sum((bias2[:, :128] + bias2[:, 128:]).T, axis=0, keepdims=True)
    sums[ROW_BIAS:] = jnp.concatenate(
        [inner_row_sum, hidden_row_sum, jnp.zeros((SUM_ROWS - ROW_BIAS - 2, 128), F32)], 0
    )


def field_extended(inside, south_tile, north_tile, second, west_tile, east_tile, lane_start, wide):
    tall = rows_extended(inside, south_tile, north_tile, second)
    return jnp.concatenate([tall, edge_columns(west_tile, east_tile, lane_start, wide)], axis=1)


def gram_kernel(
    zonal, meridian, sea, depth, south_edge, north_edge, west_edge, east_edge, west_corner, east_corner,
    sums,
    basis, parts, east_open, north_open,
    east_transport, north_transport, east_bits, north_bits,
):
    west_tile = with_corners(west_edge, west_corner)
    east_tile = with_corners(east_edge, east_corner)

    def extended(inside, index, second, lane_start):
        return field_extended(
            inside, south_edge[index], north_edge[index], second,
            west_tile, east_tile, lane_start, WIDE,
        )

    def gather(k):
        wet = extended(sea[k].astype(F32), LEVELS + k, True, WET_LANE + WIDE * k)
        east_pair = wet * east(wet)
        north_pair = wet * north(wet)
        east_transport[...] += east_pair * extended(
            zonal[k], LEVELS + k, False, ZONAL_LANE + WIDE * k
        )
        north_transport[...] += north_pair * extended(
            meridian[k], k, True, MERIDIAN_LANE + WIDE * k
        )
        place_value = float(1 << k)
        east_bits[...] += east_pair[8 : ROWS + 8] * place_value
        north_bits[...] += north_pair[:, :COLS] * place_value

    for total in (east_transport, north_transport, east_bits, north_bits):
        total[...] = jnp.zeros_like(total)
    for k in range(LEVELS):
        gather(k)
    east_open[...] = east_bits[...].astype(jnp.int32)
    north_open[...] = north_bits[...].astype(jnp.int32)
    source = -(
        (east_transport[...] - west(east_transport[...]))
        + (north_transport[...] - south(north_transport[...]))
    )
    floor = extended(depth[...].astype(F32), 2 * LEVELS, False, DEPTH_LANE)
    east_depth = jnp.minimum(floor, east(floor))
    north_depth = jnp.minimum(floor, north(floor))
    west_depth = west(east_depth)
    south_depth = south(north_depth)

    def operate(field):
        return (
            SIGMA * field
            + east_depth * (field - east(field))
            + west_depth * (field - west(field))
            + north_depth * (field - north(field))
            + south_depth * (field - south(field))
        )

    image0 = operate(source)
    first = (image0 - CENTRE * source) * (1.0 / HALF_WIDTH)
    image1 = operate(first)
    second = (image1 - CENTRE * first) * (2.0 / HALF_WIDTH) - source
    image2 = operate(second)
    basis[0] = source
    basis[1] = first
    basis[2] = second

    lane = iota((1, 128), 1)
    gram = jnp.zeros((1, 128), F32)
    pairs = (
        (source, image0), (first, image0), (second, image0),
        (first, image1), (second, image1), (second, image2),
        (source, source), (first, source), (second, source),
    )
    for i, (a, b) in enumerate(pairs):
        total = jnp.sum(a[8 : ROWS + 8, :COLS] * b[8 : ROWS + 8, :COLS], axis=0, keepdims=True)
        gram = jnp.where(lane == i, jnp.sum(total, axis=1, keepdims=True), gram)
    count, tall, _ = parts.shape
    own = SUM_ROWS // count
    tail = jnp.broadcast_to(gram, (tall - own, 128))
    for i in range(count):
        parts[i, :own] = sums[i * own : (i + 1) * own]
        parts[i, own:] = tail


def galerkin(h00, h01, h02, h11, h12, h22, g0, g1, g2):
    tiny = 1e-6

    def pivot(value, scale):
        good = value > tiny * scale
        return jnp.where(good, 1.0 / jnp.where(good, value, 1.0), 0.0)

    p0 = pivot(h00, 0.0)
    l10 = h01 * p0
    l20 = h02 * p0
    d1 = h11 - l10 * h01
    p1 = pivot(d1, h11)
    s21 = h12 - l20 * h01
    l21 = s21 * p1
    d2 = h22 - l20 * h02 - l21 * s21
    p2 = pivot(d2, h22)
    z0 = g0
    z1 = g1 - l10 * z0
    z2 = g2 - l20 * z0 - l21 * z1
    y2 = z2 * p2
    y1 = z1 * p1 - l21 * y2
    y0 = z0 * p0 - l10 * y1 - l20 * y2
    return y0, y1, y2


def final_kernel(
    scale, zonal, meridian, base, east_face, north_face, south_edge, west_edge, basis, east_open, north_open,
    parts,
    revised_far, height_out, grad1, bias1, grad2, bias2, grad3, bias3,
    revised, falls, totals, sent,
):
    def store(k):
        return pltpu.make_async_copy(revised.at[k], revised_far.at[k], sent.at[k])

    count = parts.shape[0]
    own = SUM_ROWS // count
    gram = parts[0, own : own + 1]
    y0, y1, y2 = galerkin(*[gram[:, i : i + 1] for i in range(9)])
    height = y0 * basis[0] + y1 * basis[1] + y2 * basis[2]
    height_out[...] = height[8 : ROWS + 8, :COLS]
    falls[0] = east(height) - height
    falls[1] = north(height) - height
    tall = ROWS + 8

    def level(k):
        bit = 1 << k
        u = jnp.concatenate([zonal[k], turn(west_edge[...], 128 - WIDE - ZONAL_LANE - WIDE * k, 1)], 1)
        v = jnp.concatenate([turn(south_edge[k], 4, 0), meridian[k]], 0)
        flux = jnp.where((east_open[...] & bit) != 0, (u - falls[0, 8 : ROWS + 8]) * east_face[k], 0.0)
        spread = (flux - west(flux))[:, :COLS]
        flux = jnp.where((north_open[:tall] & bit) != 0, (v - falls[1, :tall, :COLS]) * north_face[k], 0.0)
        spread = spread + (flux - south(flux))[8:]
        revised[k] = base[k] - spread
        store(k).start()

    for k in range(LEVELS):
        level(k)
    for i in range(count):
        totals[i * own : (i + 1) * own] = parts[i, :own] * scale
    grad2[...] = totals[0:HID]
    grad1[...] = totals[ROW_INNER : ROW_INNER + FIN]
    grad3[...] = totals[ROW_OUTER : ROW_OUTER + LEVELS]
    bias1[...] = totals[ROW_BIAS : ROW_BIAS + 1]
    bias2[...] = totals[ROW_BIAS + 1 : ROW_BIAS + 2]
    outer_bias = jnp.sum(totals[ROW_OUTER_BIAS : ROW_OUTER_BIAS + LEVELS], axis=1, keepdims=True)
    diagonal = iota((LEVELS, LEVELS), 0) == iota((LEVELS, LEVELS), 1)
    bias3[...] = jnp.sum(jnp.where(diagonal, outer_bias, 0.0), axis=0, keepdims=True)
    for k in range(LEVELS):
        store(k).wait()


def struct(*shape, dtype=F32):
    return jax.ShapeDtypeStruct(shape, dtype)


def call(kernel, out_shape, scratch=(), mib=16, flops=0, transcendentals=0, nbytes=0, **specs):
    return pl.pallas_call(
        kernel,
        out_shape=out_shape,
        scratch_shapes=list(scratch),
        compiler_params=pltpu.CompilerParams(vmem_limit_bytes=mib * 1024 * 1024),
        cost_estimate=pl.CostEstimate(
            flops=flops, transcendentals=transcendentals, bytes_accessed=nbytes
        ),
        **specs,
    )


def near(count):
    return [pl.BlockSpec(memory_space=pltpu.VMEM)] * count


def far(count):
    return [pl.BlockSpec(memory_space=pltpu.HBM)] * count


def sum_kernel(parts, copies):
    total = parts[0]
    for i in range(1, parts.shape[0]):
        total = total + parts[i]
    for i in range(copies.shape[0]):
        copies[i] = total


def summed_copies(parts, count):
    return call(sum_kernel, struct(count, *parts.shape[1:]), mib=4, nbytes=300_000)(parts)


def local(thermal, zonal, meridian, sea, depth, adjoint, w1, b1, w2, b2, w3, b3):
    lons, lats = lax.axis_size("lon"), lax.axis_size("lat")
    ring = [(i, (i + 1) % lons) for i in range(lons)]
    line = [(i, i + 1) for i in range(lats - 1)]

    def back(pairs):
        return [(target, source) for source, target in pairs]

    to_north, to_south = call(
        pack_rows_kernel,
        (struct(17, 8, COLS), struct(17, 8, COLS)),
        scratch=[
            pltpu.VMEM((6, LEVELS, 8, COLS), F32),
            pltpu.VMEM((2, LEVELS, 8, COLS), jnp.int32),
            pltpu.VMEM((2, 8, COLS), jnp.int32),
            pltpu.SemaphoreType.DMA((10,)),
        ],
        in_specs=far(5),
        mib=58,
        nbytes=1_000_000,
    )(thermal, zonal, meridian, sea, depth)
    south_edge = lax.ppermute(to_north, "lat", line)
    north_edge = lax.ppermute(to_south, "lat", back(line))
    high, low = call(
        pack_columns_kernel,
        (struct(ROWS, 128), struct(ROWS, 128)),
        mib=8,
        flops=4_000_000,
        nbytes=5_000_000,
    )(thermal, zonal, meridian, sea, depth)
    west_edge = lax.ppermute(high, "lon", ring)
    east_edge = lax.ppermute(low, "lon", back(ring))
    to_east, to_west = call(
        pack_corners_kernel,
        (struct(16, 128), struct(16, 128)),
        mib=4,
        nbytes=400_000,
    )(south_edge, north_edge)
    west_corner = lax.ppermute(to_east, "lon", ring)
    east_corner = lax.ppermute(to_west, "lon", back(ring))

    base, east_face, north_face, sums = call(
        closure_kernel,
        (
            struct(LEVELS, ROWS, COLS),
            struct(LEVELS, ROWS, EXT_COLS),
            struct(LEVELS, ROWS + 8, COLS),
            struct(SUM_ROWS, 128),
        ),
        scratch=[
            pltpu.VMEM((LEVELS, EXT_ROWS, COLS), F32),
            pltpu.VMEM((LEVELS, ROWS, 128), F32),
            pltpu.VMEM((8 * (HID + FIN), 8 * FIN), BF16),
            pltpu.VMEM((2 * HID, 2 * HID), BF16),
            pltpu.VMEM((2 * HID, 2 * HID), BF16),
            pltpu.VMEM((64, 8 * HID), BF16),
            pltpu.VMEM((8 * HID, 64), BF16),
            pltpu.VMEM((HID, COLS), F32),
            pltpu.VMEM((HID, COLS), F32),
        ]
        + 2
        * [
            pltpu.VMEM((8 * HID, COLS), BF16),
            pltpu.VMEM((8, HID + FIN, COLS), BF16),
            pltpu.VMEM((8 * HID, COLS), BF16),
            pltpu.VMEM((8, HID, COLS), F32),
            pltpu.VMEM((8, HID, COLS), F32),
            pltpu.VMEM((LEVELS, 8, COLS), F32),
        ]
        + [
            pltpu.VMEM((HID + FIN, COLS), F32),
            pltpu.VMEM((64, 8 * HID), F32),
            pltpu.VMEM((HID, COLS), F32),
            pltpu.VMEM((HID, COLS), F32),
            pltpu.VMEM((LEVELS, 8, COLS), F32),
        ],
        in_specs=near(13) + [pl.BlockSpec(memory_space=pltpu.SMEM)],
        mib=24,
        flops=8_000_000_000,
        transcendentals=9_000_000,
        nbytes=5_000_000,
    )(
        thermal, sea, depth, adjoint, south_edge, north_edge, west_edge, east_edge,
        w1.T, b1[None], w2, b2[None], w3, b3,
    )
    basis, parts, east_open, north_open = call(
        gram_kernel,
        (
            struct(3, EXT_ROWS, EXT_COLS),
            struct(lons, (SUM_ROWS // lons // 8 + 1) * 8, 128),
            struct(ROWS, EXT_COLS, dtype=jnp.int32),
            struct(EXT_ROWS, COLS, dtype=jnp.int32),
        ),
        scratch=[pltpu.VMEM((EXT_ROWS, EXT_COLS), F32)] * 2
        + [pltpu.VMEM((ROWS, EXT_COLS), F32), pltpu.VMEM((EXT_ROWS, COLS), F32)],
        flops=20_000_000,
        nbytes=5_000_000,
    )(
        zonal, meridian, sea, depth, south_edge, north_edge, west_edge, east_edge, west_corner, east_corner,
        sums,
    )
    parts = lax.all_to_all(parts, "lon", 0, 0)
    parts = lax.all_to_all(summed_copies(parts, lats), "lat", 0, 0)
    parts = lax.all_to_all(summed_copies(parts, lons), "lon", 0, 0)
    scale = GRADIENT_GAIN / math.sqrt(ROWS * lats * COLS * lons)
    revised, height, grad1, bias1, grad2, bias2, grad3, bias3 = call(
        functools.partial(final_kernel, scale),
        (
            struct(LEVELS, ROWS, COLS),
            struct(ROWS, COLS),
            struct(FIN, HID),
            struct(1, HID),
            struct(HID, HID),
            struct(1, HID),
            struct(LEVELS, HID),
            struct(1, LEVELS),
        ),
        scratch=[
            pltpu.VMEM((LEVELS, ROWS, COLS), F32),
            pltpu.VMEM((2, EXT_ROWS, EXT_COLS), F32),
            pltpu.VMEM((SUM_ROWS, 128), F32),
            pltpu.SemaphoreType.DMA((LEVELS,)),
        ],
        out_specs=tuple(far(1) + near(7)),
        flops=20_000_000,
        nbytes=8_000_000,
    )(
        zonal, meridian, base, east_face, north_face, south_edge, west_edge, basis, east_open, north_open, parts,
    )
    return (
        revised,
        height,
        grad1.T,
        bias1.reshape(HID),
        grad2,
        bias2.reshape(HID),
        grad3,
        bias3.reshape(LEVELS),
    )


def solution(mesh):
    cube, plane, whole = P(None, "lat", "lon"), P("lat", "lon"), P()
    return jax.shard_map(
        local,
        mesh=mesh,
        in_specs=(cube, cube, cube, cube, plane, cube) + (whole,) * 6,
        out_specs=(cube, plane) + (whole,) * 6,
        check_vma=False,
    )
```
